32 devices in a mesh: band: 16 (over z, y, x), group: 2 (over core).
Axes of the slice: x: 2, y: 2, z: 4, core: 2. Of those that a mesh axis runs over, the one named last changes fastest.
Arguments:
- trial: bfloat16 [16, 64, 4096], P('band'), may hold values from -6 to 6
- orbitals: bfloat16 [32, 64, 4096], P(('band', 'group')), may hold values from -6 to 6
- labels: int32 [32], P(('band', 'group')), may hold values from 0 to 31, each once
- kernel_mask: int32 [64, 4096], replicated, may hold values from 0 to 1, as said below
Outputs:
- exchange_field: float32 [16, 64, 4096], P('band', 'group')
The draws below stay inside these ranges and needn't reach their ends.
Inputs may be any that keep to these rules, and one draw needn't show every extreme that they name: `labels`: a permutation of the source orbitals' numbers. `kernel_mask`: unchanged when any one frequency index k is replaced by (64 - k) mod 64.
All inputs are finite; a program needn't handle non-finite values.
Results may differ from the reference program's by a relative error of at most 0.009.
Values may be sent and summed in bfloat16 or wider, within the bound.
A program may use at most 64 MiB of HBM per device.

```python
import jax
import jax.numpy as jnp
from jax import lax

GRID = 64
WINDOW = 2
NORB = 32
N_BAND = 16
N_GROUP = 2


def draw_kernel_mask(key, part):
    half_size = GRID // 2 + 1
    random_bits = jax.random.randint(key, (half_size, half_size, half_size), 0, 4)
    kept_mask = jnp.where(random_bits > 0, 1, 0).astype(jnp.int32)
    frequency = jnp.arange(GRID, dtype=jnp.int32)
    folded = jnp.minimum(frequency, GRID - frequency)
    cube = kept_mask[folded][:, folded][:, :, folded]
    return cube.reshape(GRID, GRID * GRID)


def level_of(rng, shape, cuts, smallest, top_value):
    factor_of = 1.0
    for dim, shards_of in cuts:
        steps = jax.random.uniform(jax.random.fold_in(jax.random.fold_in(rng, 6), dim), (shards_of,), jnp.float32, smallest / len(cuts), top_value / len(cuts))
        factor_of = factor_of * jnp.repeat(jnp.exp(steps), shape[dim] // shards_of).reshape((-1,) + (1,) * (len(shape) - 1 - dim))
    return factor_of


def noise(rng, dims, deviation, limit, pieces=(), held_as=jnp.bfloat16):
    drawn = deviation * jax.random.normal(rng, dims, jnp.float32)
    if pieces:
        drawn = drawn * level_of(rng, dims, pieces, -0.22, 0.18)
    return jnp.clip(drawn, -limit, limit).astype(held_as)


def setup_inputs(seed: int = 0) -> dict:
    key_list = jax.random.split(jax.random.key(seed), 5)
    trial = noise(key_list[0], (N_BAND, GRID, GRID * GRID), 1.0, 6.0, ((0, 16),))
    orbitals = noise(key_list[1], (NORB, GRID, GRID * GRID), 1.0, 6.0, ((0, 32),))
    labels = jax.random.permutation(key_list[2], NORB).astype(jnp.int32)
    kernel_mask = draw_kernel_mask(jax.random.fold_in(key_list[4], 71), 0)
    return {"trial": trial, "orbitals": orbitals, "labels": labels, "kernel_mask": kernel_mask}


screen_square = 16.0

def cas_table(grid_size):
    frequency = jnp.arange(grid_size, dtype=jnp.int32)
    product = frequency[:, None] * frequency[None, :] % grid_size
    phase_angle = product.astype(jnp.float32) * (2.0 * jnp.pi / grid_size)
    return ((jnp.cos(phase_angle) + jnp.sin(phase_angle)) / jnp.sqrt(jnp.float32(grid_size))).astype(jnp.bfloat16)

def screened_kernel(mask_cube):
    grid_size = mask_cube.shape[0]
    frequency = jnp.arange(grid_size, dtype=jnp.int32)
    signed = jnp.where(frequency < grid_size // 2, frequency, frequency - grid_size)
    squared = signed * signed
    q_square = squared[:, None, None] + squared[None, :, None] + squared[None, None, :]
    return mask_cube.astype(jnp.float32) * screen_square / (q_square.astype(jnp.float32) + screen_square)

def occupation(label_values, orbital_count):
    shifted = (label_values.astype(jnp.float32) - orbital_count / 2.0) / (orbital_count / 4.0)
    return 1.0 / (1.0 + jnp.exp(shifted))

def axis_pass(field_data, hartley):
    return jnp.einsum('pxyz,xk->pyzk', field_data.astype(jnp.float32), hartley.astype(jnp.float32), precision=lax.Precision.HIGHEST)

def reference(trial, orbitals, labels, kernel_mask):
    grid_size = GRID
    band_count = N_BAND
    group_count = N_GROUP
    hartley = cas_table(grid_size)
    kernel = screened_kernel(kernel_mask.reshape(grid_size, grid_size, grid_size))
    weights = occupation(labels, band_count * group_count).reshape(band_count, group_count)
    source_cube = orbitals.reshape(band_count, group_count, grid_size, grid_size, grid_size)
    target_cube = trial.reshape(band_count, grid_size, grid_size, grid_size)

    def one_target(band_index):
        positions = (band_index + jnp.arange(WINDOW, dtype=jnp.int32)) % band_count
        sources = jnp.take(source_cube, positions, axis=0).reshape(WINDOW * group_count, grid_size, grid_size, grid_size)
        source_weights = jnp.take(weights, positions, axis=0).reshape(-1)
        target = lax.dynamic_index_in_dim(target_cube, band_index, 0, keepdims=False)
        density = (target.astype(jnp.float32)[None] * sources.astype(jnp.float32)).astype(jnp.bfloat16)
        first = axis_pass(density, hartley).astype(jnp.bfloat16)
        second = axis_pass(first, hartley).astype(jnp.bfloat16)
        spectrum = (axis_pass(second, hartley) * kernel[None]).astype(jnp.bfloat16)
        back_first = axis_pass(spectrum, hartley).astype(jnp.bfloat16)
        back_second = axis_pass(back_first, hartley).astype(jnp.bfloat16)
        potential = axis_pass(back_second, hartley)
        contribution = source_weights[:, None, None, None] * potential * sources.astype(jnp.float32)
        return -lax.optimization_barrier(jnp.sum(contribution, axis=0)).reshape(grid_size, grid_size * grid_size)
    return lax.map(one_target, jnp.arange(band_count, dtype=jnp.int32))
```

```python
import functools

import jax
import jax.numpy as jnp
import ml_dtypes
import numpy as np
from jax import lax
from jax.experimental import pallas as pl
from jax.experimental.pallas import tpu as pltpu
from jax.sharding import PartitionSpec as P

screen_square = 16.0

STACK = 4
PAD = 8


def cas_blocks(grid_size):
    frequency = np.arange(grid_size)
    angle = (np.outer(frequency, frequency) % grid_size) * (2.0 * np.pi / grid_size)
    table = (np.cos(angle) + np.sin(angle)) / np.sqrt(grid_size)
    blocks = np.kron(np.eye(STACK), table).astype(np.float32)
    return jnp.asarray(blocks.astype(ml_dtypes.bfloat16))


def occupation(label_values, orbital_count):
    shifted = (label_values.astype(jnp.float32) - orbital_count / 2.0) / (orbital_count / 4.0)
    return 1.0 / (1.0 + jnp.exp(shifted))


def signed_square(index, grid_size):
    signed = jnp.where(index < grid_size // 2, index, index - grid_size)
    return (signed * signed).astype(jnp.float32)


def exchange_kernel(
    n, bands, groups,
    trial_hbm, orbital_hbm, label_ref, mask_hbm, blocks_ref, out_ref,
    target, own, other, mask, cube, coulomb, field, label_own, label_other,
    give, take, local_sem, send_sem, recv_sem, label_send, label_recv, give_sem, take_sem,
):
    band, group = lax.axis_index("band"), lax.axis_index("group")
    before = lax.rem(band + bands - 1, bands)
    after = lax.rem(band + 1, bands)
    half, lanes, wide = n // 2, 2 * n, STACK * n
    chunk = STACK * wide
    chunks = n * n // chunk
    planes = chunk // n
    pitch = n + PAD
    rows = n // groups
    mesh_id = pl.DeviceIdType.MESH

    def columns(c):
        return pl.ds(c * chunk, chunk)

    local = [
        pltpu.make_async_copy(orbital_hbm.at[0], own, local_sem.at[0]),
        pltpu.make_async_copy(trial_hbm.at[0], target, local_sem.at[1]),
        pltpu.make_async_copy(mask_hbm, mask, local_sem.at[2]),
    ]
    for copy in local:
        copy.start()
    label_own[...] = jnp.full(label_own.shape, label_ref[0], jnp.int32)

    barrier = pltpu.get_barrier_semaphore()
    peers = [lax.rem(group + k, groups) for k in range(1, groups)]
    for neighbour in (before, after):
        pl.semaphore_signal(barrier, inc=1, device_id={"band": neighbour}, device_id_type=mesh_id)
    for peer in peers:
        pl.semaphore_signal(barrier, inc=1, device_id={"group": peer}, device_id_type=mesh_id)
    pl.semaphore_wait(barrier, 2 + len(peers))

    sent = []
    for c in range(chunks):
        sent.append(pltpu.make_async_remote_copy(
            src_ref=orbital_hbm.at[0, :, columns(c)], dst_ref=other.at[:, columns(c)],
            send_sem=send_sem.at[c], recv_sem=recv_sem.at[c],
            device_id={"band": before}, device_id_type=mesh_id))
        sent[-1].start()
    label_copy = pltpu.make_async_remote_copy(
        src_ref=label_own, dst_ref=label_other, send_sem=label_send, recv_sem=label_recv,
        device_id={"band": before}, device_id_type=mesh_id)
    label_copy.start()

    blocks = blocks_ref[...]
    left = lax.broadcasted_iota(jnp.int32, (half, lanes), 1) < n

    def matmul(a, b):
        return jnp.dot(a, b, preferred_element_type=jnp.float32)

    def exchanged(value):
        low, high = value[:half], value[half:]
        first = jnp.where(left, low, pltpu.roll(high, n, 1))
        second = jnp.where(left, pltpu.roll(low, n, 1), high)
        return first, second

    def restored(first, second):
        low = jnp.where(left, first, pltpu.roll(second, n, 1))
        high = jnp.where(left, pltpu.roll(first, n, 1), second)
        return jnp.concatenate([low, high], axis=0)

    def put_planes(ref, plane, value):
        for step, part in enumerate(exchanged(value)):
            ref[pl.ds(plane + step, half, stride=pitch), :] = part

    def forward(c, source):
        pieces = []
        for q in range(STACK):
            place = pl.ds(c * chunk + q * wide, wide)
            density = target[:, place].astype(jnp.float32) * source[:, place].astype(jnp.float32)
            pieces.append(density.astype(jnp.bfloat16))
        first = matmul(blocks, jnp.concatenate(pieces, axis=0)).astype(jnp.bfloat16)
        second = matmul(first, blocks)
        for q in range(STACK):
            for h in range(wide // lanes):
                put_planes(cube, c * planes + q * STACK + 2 * h,
                           second[q * n:(q + 1) * n, h * lanes:(h + 1) * lanes])

    def middle():
        for start in range(0, half, 2 * STACK):
            def gathered(ref):
                return jnp.concatenate([
                    jnp.concatenate([
                        ref[pl.ds((start + side * STACK + q) * pitch, n), :] for q in range(STACK)
                    ], axis=0) for side in range(2)
                ], axis=1)
            spectrum = matmul(blocks, gathered(cube).astype(jnp.bfloat16)) * gathered(coulomb)
            back = matmul(blocks, spectrum.astype(jnp.bfloat16))
            for side in range(2):
                for q in range(STACK):
                    cube[pl.ds((start + side * STACK + q) * pitch, n), :] = (
                        back[q * n:(q + 1) * n, side * lanes:(side + 1) * lanes])

    def backward(c, source, weight, accumulate):
        pieces = []
        for q in range(STACK):
            pairs = []
            for h in range(wide // lanes):
                plane = c * planes + q * STACK + 2 * h
                pairs.append(restored(cube[pl.ds(plane, half, stride=pitch), :],
                                      cube[pl.ds(plane + 1, half, stride=pitch), :]))
            pieces.append(jnp.concatenate(pairs, axis=1).astype(jnp.bfloat16))
        back = matmul(blocks, jnp.concatenate(pieces, axis=0)).astype(jnp.bfloat16)
        potential = matmul(back, blocks)
        for q in range(STACK):
            place = pl.ds(c * chunk + q * wide, wide)
            part = weight * potential[q * n:(q + 1) * n] * source[:, place].astype(jnp.float32)
            field[:, place] = field[:, place] + part if accumulate else part

    local[2].wait()
    ky_lane = lax.broadcasted_iota(jnp.int32, (n, lanes), 1)
    kx_row = lax.broadcasted_iota(jnp.int32, (n, lanes), 0)
    base = signed_square(kx_row, n) + signed_square(lax.rem(ky_lane, n), n) + screen_square
    for t in range(n // 2):
        ky = 2 * t + jnp.where(ky_lane < n, 0, 1)
        kept = mask[:, pl.ds(t * lanes, lanes)].astype(jnp.float32)
        put_planes(coulomb, 2 * t, kept * (screen_square / (base + signed_square(ky, n))))

    local[0].wait()
    local[1].wait()
    orbital_count = bands * groups
    for c in range(chunks):
        forward(c, own)
    middle()
    weight = occupation(label_own[0:1, :], orbital_count)
    for c in range(chunks):
        backward(c, own, weight, False)

    for c in range(chunks):
        sent[c].wait_recv()
        forward(c, other)
    middle()
    label_copy.wait_recv()
    weight = occupation(label_other[0:1, :], orbital_count)
    passed = []
    for c in range(chunks):
        backward(c, other, weight, True)
        for k, peer in enumerate(peers):
            give[k, :, columns(c)] = field[pl.ds(pl.multiple_of(peer * rows, rows), rows), columns(c)].astype(jnp.bfloat16)
            copy = pltpu.make_async_remote_copy(
                src_ref=give.at[k, :, columns(c)], dst_ref=take.at[k, :, columns(c)],
                send_sem=give_sem.at[k, c], recv_sem=take_sem.at[k, c],
                device_id={"group": peer}, device_id_type=mesh_id)
            copy.start()
            passed.append((c, k, copy))
    for c in range(chunks):
        total = field[pl.ds(pl.multiple_of(group * rows, rows), rows), columns(c)]
        for at, k, copy in passed:
            if at == c:
                copy.wait_recv()
                total = total + take[k, :, columns(c)].astype(jnp.float32)
        out_ref[0, :, columns(c)] = -total
    for _, _, copy in passed:
        copy.wait_send()
    for copy in sent:
        copy.wait_send()
    label_copy.wait_send()


def shards(trial, orbitals, labels, kernel_mask):
    n = trial.shape[1]
    bands, groups = lax.axis_size("band"), lax.axis_size("group")
    rows = n // groups
    chunks = n // (STACK * STACK)
    peers = groups - 1
    vmem = pl.BlockSpec(memory_space=pltpu.VMEM)
    anywhere = pl.BlockSpec(memory_space=pl.ANY)
    dma = pltpu.SemaphoreType.DMA
    return pl.pallas_call(
        functools.partial(exchange_kernel, n, bands, groups),
        out_shape=jax.ShapeDtypeStruct((1, rows, n * n), jnp.float32),
        in_specs=[anywhere, anywhere, pl.BlockSpec(memory_space=pltpu.SMEM), anywhere, vmem],
        out_specs=vmem,
        scratch_shapes=[
            pltpu.VMEM((n, n * n), jnp.bfloat16),
            pltpu.VMEM((n, n * n), jnp.bfloat16),
            pltpu.VMEM((n, n * n), jnp.bfloat16),
            pltpu.VMEM((n, n * n), jnp.int32),
            pltpu.VMEM((n // 2 * (n + PAD), 2 * n), jnp.float32),
            pltpu.VMEM((n // 2 * (n + PAD), 2 * n), jnp.float32),
            pltpu.VMEM((n, n * n), jnp.float32),
            pltpu.VMEM((8, STACK * n), jnp.int32),
            pltpu.VMEM((8, STACK * n), jnp.int32),
            pltpu.VMEM((peers, rows, n * n), jnp.bfloat16),
            pltpu.VMEM((peers, rows, n * n), jnp.bfloat16),
            dma((3,)), dma((chunks,)), dma((chunks,)), dma, dma, dma((peers, chunks)), dma((peers, chunks)),
        ],
        compiler_params=pltpu.CompilerParams(
            collective_id=0, has_side_effects=True, vmem_limit_bytes=40 * 1024 * 1024),
        name="exchange",
    )(trial, orbitals, labels, kernel_mask, cas_blocks(n))


def solution(mesh):
    in_specs = (P("band", None, None), P(("band", "group"), None, None), P(("band", "group")), P())
    out_specs = P("band", "group", None)
    return jax.shard_map(shards, mesh=mesh, in_specs=in_specs, out_specs=out_specs, check_vma=False)
```

```python
import functools

import jax
import jax.numpy as jnp
import ml_dtypes
import numpy as np
from jax import lax
from jax.experimental import pallas as pl
from jax.experimental.pallas import tpu as pltpu
from jax.sharding import PartitionSpec as P

screen_square = 16.0

STACK = 4
PAD = 8


def cas_blocks(grid_size):
    frequency = np.arange(grid_size)
    angle = (np.outer(frequency, frequency) % grid_size) * (2.0 * np.pi / grid_size)
    table = (np.cos(angle) + np.sin(angle)) / np.sqrt(grid_size)
    blocks = np.kron(np.eye(STACK), table).astype(np.float32)
    return jnp.asarray(blocks.astype(ml_dtypes.bfloat16))


def occupation(label_values, orbital_count):
    shifted = (label_values.astype(jnp.float32) - orbital_count / 2.0) / (orbital_count / 4.0)
    return 1.0 / (1.0 + jnp.exp(shifted))


def signed_square(index, grid_size):
    signed = jnp.where(index < grid_size // 2, index, index - grid_size)
    return (signed * signed).astype(jnp.float32)


def exchange_kernel(
    n, bands, groups,
    trial_hbm, orbital_hbm, label_ref, mask_hbm, blocks_hbm, out_ref,
    table, target, own, other, mask, cube, coulomb, field, label_own, label_other,
    give, take, local_sem, send_sem, recv_sem, label_send, label_recv, give_sem, take_sem,
):
    band, group = lax.axis_index("band"), lax.axis_index("group")
    before = lax.rem(band + bands - 1, bands)
    after = lax.rem(band + 1, bands)
    half, lanes, wide = n // 2, 2 * n, STACK * n
    chunk = STACK * wide
    chunks = n * n // chunk
    planes = chunk // n
    pitch = n + PAD
    rows = n // groups
    mesh_id = pl.DeviceIdType.MESH

    def columns(c):
        return pl.ds(c * chunk, chunk)

    local = [
        pltpu.make_async_copy(orbital_hbm.at[0], own, local_sem.at[0]),
        pltpu.make_async_copy(trial_hbm.at[0], target, local_sem.at[1]),
        pltpu.make_async_copy(mask_hbm, mask, local_sem.at[2]),
        pltpu.make_async_copy(blocks_hbm, table, local_sem.at[3]),
    ]
    label_own[...] = jnp.full(label_own.shape, label_ref[0], jnp.int32)

    barrier = pltpu.get_barrier_semaphore()
    peers = [lax.rem(group + k, groups) for k in range(1, groups)]
    for neighbour in (before, after):
        pl.semaphore_signal(barrier, inc=1, device_id={"band": neighbour}, device_id_type=mesh_id)
    for peer in peers:
        pl.semaphore_signal(barrier, inc=1, device_id={"group": peer}, device_id_type=mesh_id)
    pl.semaphore_wait(barrier, 2 + len(peers))

    sent = []
    for c in range(chunks):
        sent.append(pltpu.make_async_remote_copy(
            src_ref=orbital_hbm.at[0, :, columns(c)], dst_ref=other.at[:, columns(c)],
            send_sem=send_sem.at[c], recv_sem=recv_sem.at[c],
            device_id={"band": before}, device_id_type=mesh_id))
        sent[-1].start()
    label_copy = pltpu.make_async_remote_copy(
        src_ref=label_own, dst_ref=label_other, send_sem=label_send, recv_sem=label_recv,
        device_id={"band": before}, device_id_type=mesh_id)
    label_copy.start()
    for at in (2, 0, 1, 3):
        local[at].start()

    left = lax.broadcasted_iota(jnp.int32, (half, lanes), 1) < n

    def matmul(a, b):
        return jnp.dot(a, b, preferred_element_type=jnp.float32)

    def exchanged(value):
        low, high = value[:half], value[half:]
        first = jnp.where(left, low, pltpu.roll(high, n, 1))
        second = jnp.where(left, pltpu.roll(low, n, 1), high)
        return first, second

    def restored(first, second):
        low = jnp.where(left, first, pltpu.roll(second, n, 1))
        high = jnp.where(left, pltpu.roll(first, n, 1), second)
        return jnp.concatenate([low, high], axis=0)

    def put_planes(ref, plane, value):
        for step, part in enumerate(exchanged(value)):
            ref[pl.ds(plane + step, half, stride=pitch), :] = part

    def forward(c, source):
        pieces = []
        for q in range(STACK):
            place = pl.ds(c * chunk + q * wide, wide)
            pieces.append(target[:, place] * source[:, place])
        first = matmul(blocks, jnp.concatenate(pieces, axis=0)).astype(jnp.bfloat16)
        second = matmul(first, blocks)
        for q in range(STACK):
            for h in range(wide // lanes):
                put_planes(cube, c * planes + q * STACK + 2 * h,
                           second[q * n:(q + 1) * n, h * lanes:(h + 1) * lanes])

    def middle():
        for start in range(0, half, 2 * STACK):
            def gathered(ref):
                return jnp.concatenate([
                    jnp.concatenate([
                        ref[pl.ds((start + side * STACK + q) * pitch, n), :] for q in range(STACK)
                    ], axis=0) for side in range(2)
                ], axis=1)
            spectrum = matmul(blocks, gathered(cube).astype(jnp.bfloat16)) * gathered(coulomb)
            back = matmul(blocks, spectrum.astype(jnp.bfloat16))
            for side in range(2):
                for q in range(STACK):
                    cube[pl.ds((start + side * STACK + q) * pitch, n), :] = (
                        back[q * n:(q + 1) * n, side * lanes:(side + 1) * lanes])

    def backward(c, source, weight, accumulate):
        pieces = []
        for q in range(STACK):
            pairs = []
            for h in range(wide // lanes):
                plane = c * planes + q * STACK + 2 * h
                pairs.append(restored(cube[pl.ds(plane, half, stride=pitch), :],
                                      cube[pl.ds(plane + 1, half, stride=pitch), :]))
            pieces.append(jnp.concatenate(pairs, axis=1).astype(jnp.bfloat16))
        back = matmul(blocks, jnp.concatenate(pieces, axis=0)).astype(jnp.bfloat16)
        potential = matmul(back, blocks)
        for q in range(STACK):
            place = pl.ds(c * chunk + q * wide, wide)
            part = weight * potential[q * n:(q + 1) * n] * source[:, place].astype(jnp.float32)
            field[:, place] = field[:, place] + part if accumulate else part

    local[2].wait()
    ky_lane = lax.broadcasted_iota(jnp.int32, (n, lanes), 1)
    kx_row = lax.broadcasted_iota(jnp.int32, (n, lanes), 0)
    base = signed_square(kx_row, n) + signed_square(lax.rem(ky_lane, n), n) + screen_square
    for t in range(n // 2):
        ky = 2 * t + jnp.where(ky_lane < n, 0, 1)
        kept = mask[:, pl.ds(t * lanes, lanes)].astype(jnp.float32)
        put_planes(coulomb, 2 * t, kept * (screen_square / (base + signed_square(ky, n))))

    local[0].wait()
    local[1].wait()
    local[3].wait()
    blocks = table[...]
    orbital_count = bands * groups
    for c in range(chunks):
        forward(c, own)
    middle()
    weight = occupation(label_own[0:1, :], orbital_count)
    for c in range(chunks):
        backward(c, own, weight, False)

    for c in range(chunks):
        sent[c].wait_recv()
        forward(c, other)
    middle()
    label_copy.wait_recv()
    weight = occupation(label_other[0:1, :], orbital_count)
    passed = []
    for c in range(chunks):
        backward(c, other, weight, True)
        for k, peer in enumerate(peers):
            give[k, :, columns(c)] = field[pl.ds(pl.multiple_of(peer * rows, rows), rows), columns(c)].astype(jnp.bfloat16)
            copy = pltpu.make_async_remote_copy(
                src_ref=give.at[k, :, columns(c)], dst_ref=take.at[k, :, columns(c)],
                send_sem=give_sem.at[k, c], recv_sem=take_sem.at[k, c],
                device_id={"group": peer}, device_id_type=mesh_id)
            copy.start()
            passed.append((c, k, copy))
    for c in range(chunks):
        total = field[pl.ds(pl.multiple_of(group * rows, rows), rows), columns(c)]
        for at, k, copy in passed:
            if at == c:
                copy.wait_recv()
                total = total + take[k, :, columns(c)].astype(jnp.float32)
        out_ref[0, :, columns(c)] = -total
    for _, _, copy in passed:
        copy.wait_send()
    for copy in sent:
        copy.wait_send()
    label_copy.wait_send()


def shards(trial, orbitals, labels, kernel_mask):
    n = trial.shape[1]
    bands, groups = lax.axis_size("band"), lax.axis_size("group")
    rows = n // groups
    chunks = n // (STACK * STACK)
    peers = groups - 1
    vmem = pl.BlockSpec(memory_space=pltpu.VMEM)
    hbm = pl.BlockSpec(memory_space=pltpu.HBM)
    dma = pltpu.SemaphoreType.DMA
    return pl.pallas_call(
        functools.partial(exchange_kernel, n, bands, groups),
        out_shape=jax.ShapeDtypeStruct((1, rows, n * n), jnp.float32),
        in_specs=[hbm, hbm, pl.BlockSpec(memory_space=pltpu.SMEM), hbm, hbm],
        out_specs=vmem,
        scratch_shapes=[
            pltpu.VMEM((STACK * n, STACK * n), jnp.bfloat16),
            pltpu.VMEM((n, n * n), jnp.bfloat16),
            pltpu.VMEM((n, n * n), jnp.bfloat16),
            pltpu.VMEM((n, n * n), jnp.bfloat16),
            pltpu.VMEM((n, n * n), jnp.int32),
            pltpu.VMEM((n // 2 * (n + PAD), 2 * n), jnp.float32),
            pltpu.VMEM((n // 2 * (n + PAD), 2 * n), jnp.float32),
            pltpu.VMEM((n, n * n), jnp.float32),
            pltpu.VMEM((8, STACK * n), jnp.int32),
            pltpu.VMEM((8, STACK * n), jnp.int32),
            pltpu.VMEM((peers, rows, n * n), jnp.bfloat16),
            pltpu.VMEM((peers, rows, n * n), jnp.bfloat16),
            dma((4,)), dma((chunks,)), dma((chunks,)), dma, dma, dma((peers, chunks)), dma((peers, chunks)),
        ],
        compiler_params=pltpu.CompilerParams(
            collective_id=0, has_side_effects=True, vmem_limit_bytes=63 * 1024 * 1024),
        name="exchange",
    )(trial, orbitals, labels, kernel_mask, cas_blocks(n))


def solution(mesh):
    in_specs = (P("band", None, None), P(("band", "group"), None, None), P(("band", "group")), P())
    out_specs = P("band", "group", None)
    return jax.shard_map(shards, mesh=mesh, in_specs=in_specs, out_specs=out_specs, check_vma=False)
```

```python
import functools

import jax
import jax.numpy as jnp
import ml_dtypes
import numpy as np
from jax import lax
from jax.experimental import pallas as pl
from jax.experimental.pallas import tpu as pltpu
from jax.sharding import PartitionSpec as P

screen_square = 16.0

STACK = 4
PAD = 1


def cas_blocks(grid_size):
    frequency = np.arange(grid_size)
    angle = (np.outer(frequency, frequency) % grid_size) * (2.0 * np.pi / grid_size)
    table = (np.cos(angle) + np.sin(angle)) / np.sqrt(grid_size)
    blocks = np.kron(np.eye(STACK), table).astype(np.float32)
    return jnp.asarray(blocks.astype(ml_dtypes.bfloat16))


def occupation(label_values, orbital_count):
    shifted = (label_values.astype(jnp.float32) - orbital_count / 2.0) / (orbital_count / 4.0)
    return 1.0 / (1.0 + jnp.exp(shifted))


def signed_square(index, grid_size):
    signed = jnp.where(index < grid_size // 2, index, index - grid_size)
    return (signed * signed).astype(jnp.float32)


def exchange_kernel(
    n, bands, groups,
    trial_hbm, orbital_hbm, label_ref, mask_hbm, blocks_hbm, out_ref,
    table, target, own, other, mask, cube, filtered, coulomb, field, label_own, label_other,
    give, take, local_sem, send_sem, recv_sem, label_send, label_recv, give_sem, take_sem,
):
    band, group = lax.axis_index("band"), lax.axis_index("group")
    before = lax.rem(band + bands - 1, bands)
    after = lax.rem(band + 1, bands)
    half, lanes, wide = n // 2, 2 * n, STACK * n
    chunk = STACK * wide
    chunks = n * n // chunk
    planes = chunk // n
    pitch = n + PAD
    rows = n // groups
    mesh_id = pl.DeviceIdType.MESH

    def columns(c):
        return pl.ds(c * chunk, chunk)

    local = [
        pltpu.make_async_copy(orbital_hbm.at[0], own, local_sem.at[0]),
        pltpu.make_async_copy(trial_hbm.at[0], target, local_sem.at[1]),
        pltpu.make_async_copy(mask_hbm, mask, local_sem.at[2]),
        pltpu.make_async_copy(blocks_hbm, table, local_sem.at[3]),
    ]
    label_own[...] = jnp.full(label_own.shape, label_ref[0], jnp.int32)

    barrier = pltpu.get_barrier_semaphore()
    peers = [lax.rem(group + k, groups) for k in range(1, groups)]
    for neighbour in (before, after):
        pl.semaphore_signal(barrier, inc=1, device_id={"band": neighbour}, device_id_type=mesh_id)
    for peer in peers:
        pl.semaphore_signal(barrier, inc=1, device_id={"group": peer}, device_id_type=mesh_id)
    pl.semaphore_wait(barrier, 2 + len(peers))

    sent = []
    for c in range(chunks):
        sent.append(pltpu.make_async_remote_copy(
            src_ref=orbital_hbm.at[0, :, columns(c)], dst_ref=other.at[:, columns(c)],
            send_sem=send_sem.at[c], recv_sem=recv_sem.at[c],
            device_id={"band": before}, device_id_type=mesh_id))
        sent[-1].start()
    label_copy = pltpu.make_async_remote_copy(
        src_ref=label_own, dst_ref=label_other, send_sem=label_send, recv_sem=label_recv,
        device_id={"band": before}, device_id_type=mesh_id)
    label_copy.start()
    for at in (2, 0, 1, 3):
        local[at].start()

    left = lax.broadcasted_iota(jnp.int32, (half, lanes), 1) < n

    def matmul(a, b):
        return jnp.dot(a, b, preferred_element_type=jnp.float32)

    def exchanged(value):
        low, high = value[:half], value[half:]
        first = jnp.where(left, low, pltpu.roll(high, n, 1))
        second = jnp.where(left, pltpu.roll(low, n, 1), high)
        return first, second

    def restored(first, second):
        low = jnp.where(left, first, pltpu.roll(second, n, 1))
        high = jnp.where(left, pltpu.roll(first, n, 1), second)
        return jnp.concatenate([low, high], axis=0)

    def put_planes(ref, plane, value):
        for step, part in enumerate(exchanged(value)):
            ref[pl.ds(plane + step, half, stride=pitch), :] = part

    def forward(c, source):
        pieces = []
        for q in range(STACK):
            place = pl.ds(c * chunk + q * wide, wide)
            pieces.append(target[:, place] * source[:, place])
        first = matmul(blocks, jnp.concatenate(pieces, axis=0)).astype(jnp.bfloat16)
        second = matmul(first, blocks)
        for q in range(STACK):
            for h in range(wide // lanes):
                put_planes(cube, c * planes + q * STACK + 2 * h,
                           second[q * n:(q + 1) * n, h * lanes:(h + 1) * lanes])

    def middle():
        for start in range(0, half, 2 * STACK):
            def gathered(ref):
                return jnp.concatenate([
                    jnp.concatenate([
                        ref[pl.ds((start + side * STACK + q) * pitch, n), :] for q in range(STACK)
                    ], axis=0) for side in range(2)
                ], axis=1)
            spectrum = matmul(blocks, gathered(cube).astype(jnp.bfloat16)) * gathered(coulomb)
            back = matmul(blocks, spectrum.astype(jnp.bfloat16))
            for side in range(2):
                for q in range(STACK):
                    filtered[pl.ds((start + side * STACK + q) * pitch, n), :] = (
                        back[q * n:(q + 1) * n, side * lanes:(side + 1) * lanes])

    def backward(c, source, weight, accumulate):
        pieces = []
        for q in range(STACK):
            pairs = []
            for h in range(wide // lanes):
                plane = c * planes + q * STACK + 2 * h
                pairs.append(restored(filtered[pl.ds(plane, half, stride=pitch), :],
                                      filtered[pl.ds(plane + 1, half, stride=pitch), :]))
            pieces.append(jnp.concatenate(pairs, axis=1).astype(jnp.bfloat16))
        back = matmul(blocks, jnp.concatenate(pieces, axis=0)).astype(jnp.bfloat16)
        potential = matmul(back, blocks)
        for q in range(STACK):
            place = pl.ds(c * chunk + q * wide, wide)
            part = weight * potential[q * n:(q + 1) * n] * source[:, place].astype(jnp.float32)
            field[:, place] = field[:, place] + part if accumulate else part

    local[2].wait()
    ky_lane = lax.broadcasted_iota(jnp.int32, (n, lanes), 1)
    kx_row = lax.broadcasted_iota(jnp.int32, (n, lanes), 0)
    base = signed_square(kx_row, n) + signed_square(lax.rem(ky_lane, n), n) + screen_square
    for t in range(n // 2):
        ky = 2 * t + jnp.where(ky_lane < n, 0, 1)
        kept = mask[:, pl.ds(t * lanes, lanes)].astype(jnp.float32)
        put_planes(coulomb, 2 * t, kept * (screen_square / (base + signed_square(ky, n))))

    local[0].wait()
    local[1].wait()
    local[3].wait()
    blocks = table[...]
    orbital_count = bands * groups
    for c in range(chunks):
        forward(c, own)
    middle()
    weight = occupation(label_own[0:1, :], orbital_count)
    for c in range(chunks):
        backward(c, own, weight, False)

    for c in range(chunks):
        sent[c].wait_recv()
        forward(c, other)
    middle()
    label_copy.wait_recv()
    weight = occupation(label_other[0:1, :], orbital_count)
    passed = []
    for c in range(chunks):
        backward(c, other, weight, True)
        for k, peer in enumerate(peers):
            give[k, :, columns(c)] = field[pl.ds(pl.multiple_of(peer * rows, rows), rows), columns(c)].astype(jnp.bfloat16)
            copy = pltpu.make_async_remote_copy(
                src_ref=give.at[k, :, columns(c)], dst_ref=take.at[k, :, columns(c)],
                send_sem=give_sem.at[k, c], recv_sem=take_sem.at[k, c],
                device_id={"group": peer}, device_id_type=mesh_id)
            copy.start()
            passed.append((c, k, copy))
    for c in range(chunks):
        total = field[pl.ds(pl.multiple_of(group * rows, rows), rows), columns(c)]
        for at, k, copy in passed:
            if at == c:
                copy.wait_recv()
                total = total + take[k, :, columns(c)].astype(jnp.float32)
        out_ref[0, :, columns(c)] = -total
    for _, _, copy in passed:
        copy.wait_send()
    for copy in sent:
        copy.wait_send()
    label_copy.wait_send()


def shards(trial, orbitals, labels, kernel_mask):
    n = trial.shape[1]
    bands, groups = lax.axis_size("band"), lax.axis_size("group")
    rows = n // groups
    chunks = n // (STACK * STACK)
    peers = groups - 1
    vmem = pl.BlockSpec(memory_space=pltpu.VMEM)
    hbm = pl.BlockSpec(memory_space=pltpu.HBM)
    dma = pltpu.SemaphoreType.DMA
    return pl.pallas_call(
        functools.partial(exchange_kernel, n, bands, groups),
        out_shape=jax.ShapeDtypeStruct((1, rows, n * n), jnp.float32),
        in_specs=[hbm, hbm, pl.BlockSpec(memory_space=pltpu.SMEM), hbm, hbm],
        out_specs=vmem,
        scratch_shapes=[
            pltpu.VMEM((STACK * n, STACK * n), jnp.bfloat16),
            pltpu.VMEM((n, n * n), jnp.bfloat16),
            pltpu.VMEM((n, n * n), jnp.bfloat16),
            pltpu.VMEM((n, n * n), jnp.bfloat16),
            pltpu.VMEM((n, n * n), jnp.int32),
            pltpu.VMEM((n // 2 * (n + PAD), 2 * n), jnp.float32),
            pltpu.VMEM((n // 2 * (n + PAD), 2 * n), jnp.float32),
            pltpu.VMEM((n // 2 * (n + PAD), 2 * n), jnp.float32),
            pltpu.VMEM((n, n * n), jnp.float32),
            pltpu.VMEM((8, STACK * n), jnp.int32),
            pltpu.VMEM((8, STACK * n), jnp.int32),
            pltpu.VMEM((peers, rows, n * n), jnp.bfloat16),
            pltpu.VMEM((peers, rows, n * n), jnp.bfloat16),
            dma((4,)), dma((chunks,)), dma((chunks,)), dma, dma, dma((peers, chunks)), dma((peers, chunks)),
        ],
        compiler_params=pltpu.CompilerParams(
            collective_id=0, has_side_effects=True, vmem_limit_bytes=63 * 1024 * 1024),
        name="exchange",
    )(trial, orbitals, labels, kernel_mask, cas_blocks(n))


def solution(mesh):
    in_specs = (P("band", None, None), P(("band", "group"), None, None), P(("band", "group")), P())
    out_specs = P("band", "group", None)
    return jax.shard_map(shards, mesh=mesh, in_specs=in_specs, out_specs=out_specs, check_vma=False)
```

```python
import functools

import jax
import jax.numpy as jnp
import ml_dtypes
import numpy as np
from jax import lax
from jax.experimental import pallas as pl
from jax.experimental.pallas import tpu as pltpu
from jax.sharding import PartitionSpec as P

screen_square = 16.0

STACK = 4
PAD = 1


def cas_blocks(grid_size):
    frequency = np.arange(grid_size)
    angle = (np.outer(frequency, frequency) % grid_size) * (2.0 * np.pi / grid_size)
    table = (np.cos(angle) + np.sin(angle)) / np.sqrt(grid_size)
    blocks = np.kron(np.eye(STACK), table).astype(np.float32)
    return jnp.asarray(blocks.astype(ml_dtypes.bfloat16))


def occupation(label_values, orbital_count):
    shifted = (label_values.astype(jnp.float32) - orbital_count / 2.0) / (orbital_count / 4.0)
    return 1.0 / (1.0 + jnp.exp(shifted))


def signed_square(index, grid_size):
    signed = jnp.where(index < grid_size // 2, index, index - grid_size)
    return (signed * signed).astype(jnp.float32)


def exchange_kernel(
    n, bands, groups,
    trial_hbm, orbital_hbm, label_ref, mask_hbm, blocks_hbm, out_ref,
    table, target, own, other, mask, staged, back, cube, filtered, coulomb, field, label_own, label_other,
    give, take, local_sem, send_sem, recv_sem, label_send, label_recv, give_sem, take_sem,
):
    band, group = lax.axis_index("band"), lax.axis_index("group")
    before = lax.rem(band + bands - 1, bands)
    after = lax.rem(band + 1, bands)
    half, lanes, wide = n // 2, 2 * n, STACK * n
    chunk = STACK * wide
    chunks = n * n // chunk
    planes = chunk // n
    pitch = n + PAD
    rows = n // groups
    mesh_id = pl.DeviceIdType.MESH

    def columns(c):
        return pl.ds(c * chunk, chunk)

    local = [
        pltpu.make_async_copy(orbital_hbm.at[0], own, local_sem.at[0]),
        pltpu.make_async_copy(trial_hbm.at[0], target, local_sem.at[1]),
        pltpu.make_async_copy(mask_hbm, mask, local_sem.at[2]),
        pltpu.make_async_copy(blocks_hbm, table, local_sem.at[3]),
    ]
    label_own[...] = jnp.full(label_own.shape, label_ref[0], jnp.int32)

    barrier = pltpu.get_barrier_semaphore()
    peers = [lax.rem(group + k, groups) for k in range(1, groups)]
    for neighbour in (before, after):
        pl.semaphore_signal(barrier, inc=1, device_id={"band": neighbour}, device_id_type=mesh_id)
    for peer in peers:
        pl.semaphore_signal(barrier, inc=1, device_id={"group": peer}, device_id_type=mesh_id)
    pl.semaphore_wait(barrier, 2 + len(peers))

    sent = []
    for c in range(chunks):
        sent.append(pltpu.make_async_remote_copy(
            src_ref=orbital_hbm.at[0, :, columns(c)], dst_ref=other.at[:, columns(c)],
            send_sem=send_sem.at[c], recv_sem=recv_sem.at[c],
            device_id={"band": before}, device_id_type=mesh_id))
        sent[-1].start()
    label_copy = pltpu.make_async_remote_copy(
        src_ref=label_own, dst_ref=label_other, send_sem=label_send, recv_sem=label_recv,
        device_id={"band": before}, device_id_type=mesh_id)
    label_copy.start()
    for at in (2, 0, 1, 3):
        local[at].start()

    left = lax.broadcasted_iota(jnp.int32, (half, lanes), 1) < n

    def matmul(a, b):
        return jnp.dot(a, b, preferred_element_type=jnp.float32)

    def exchanged(value):
        low, high = value[:half], value[half:]
        first = jnp.where(left, low, pltpu.roll(high, n, 1))
        second = jnp.where(left, pltpu.roll(low, n, 1), high)
        return first, second

    def restored(first, second):
        low = jnp.where(left, first, pltpu.roll(second, n, 1))
        high = jnp.where(left, pltpu.roll(first, n, 1), second)
        return jnp.concatenate([low, high], axis=0)

    def put_planes(ref, plane, value):
        for step, part in enumerate(exchanged(value)):
            ref[pl.ds(plane + step, half, stride=pitch), :] = part

    def forward(group_of_chunks, source):
        for c in group_of_chunks:
            pieces = []
            for q in range(STACK):
                place = pl.ds(c * chunk + q * wide, wide)
                pieces.append(target[:, place] * source[:, place])
            staged[pl.ds(c * wide, wide), :] = matmul(
                blocks, jnp.concatenate(pieces, axis=0)).astype(jnp.bfloat16)
        begin, count = group_of_chunks[0], len(group_of_chunks)
        second = matmul(staged[pl.ds(begin * wide, count * wide), :], blocks)
        for q in range(count * STACK):
            for h in range(wide // lanes):
                put_planes(cube, begin * planes + q * STACK + 2 * h,
                           second[q * n:(q + 1) * n, h * lanes:(h + 1) * lanes])

    def middle():
        starts = range(0, half, 2 * STACK)

        def gathered(ref, start):
            return jnp.concatenate([
                jnp.concatenate([
                    ref[pl.ds((start + side * STACK + q) * pitch, n), :] for q in range(STACK)
                ], axis=0) for side in range(2)
            ], axis=1)

        for step, start in enumerate(starts):
            spectrum = matmul(blocks, gathered(cube, start).astype(jnp.bfloat16)) * gathered(coulomb, start)
            staged[pl.ds(step * wide, wide), :] = spectrum.astype(jnp.bfloat16)
        for step, start in enumerate(starts):
            result = matmul(blocks, staged[pl.ds(step * wide, wide), :])
            for side in range(2):
                for q in range(STACK):
                    filtered[pl.ds((start + side * STACK + q) * pitch, n), :] = (
                        result[q * n:(q + 1) * n, side * lanes:(side + 1) * lanes])

    def backward_z():
        for c in range(chunks):
            for q in range(STACK):
                for h in range(wide // lanes):
                    plane = c * planes + q * STACK + 2 * h
                    pair = restored(filtered[pl.ds(plane, half, stride=pitch), :],
                                    filtered[pl.ds(plane + 1, half, stride=pitch), :])
                    staged[pl.ds(c * wide + q * n, n), pl.ds(h * lanes, lanes)] = pair.astype(jnp.bfloat16)
        back[...] = matmul(staged[...], blocks).astype(jnp.bfloat16)

    def backward_x(c, source, weight, accumulate):
        potential = matmul(blocks, back[pl.ds(c * wide, wide), :])
        for q in range(STACK):
            place = pl.ds(c * chunk + q * wide, wide)
            part = weight * potential[q * n:(q + 1) * n] * source[:, place].astype(jnp.float32)
            field[:, place] = field[:, place] + part if accumulate else part

    local[2].wait()
    ky_lane = lax.broadcasted_iota(jnp.int32, (n, lanes), 1)
    kx_row = lax.broadcasted_iota(jnp.int32, (n, lanes), 0)
    base = signed_square(kx_row, n) + signed_square(lax.rem(ky_lane, n), n) + screen_square
    for t in range(n // 2):
        ky = 2 * t + jnp.where(ky_lane < n, 0, 1)
        kept = mask[:, pl.ds(t * lanes, lanes)].astype(jnp.float32)
        put_planes(coulomb, 2 * t, kept * (screen_square / (base + signed_square(ky, n))))

    local[0].wait()
    local[1].wait()
    local[3].wait()
    blocks = table[...]
    orbital_count = bands * groups
    forward(range(chunks), own)
    middle()
    backward_z()
    weight = occupation(label_own[0:1, :], orbital_count)
    for c in range(chunks):
        backward_x(c, own, weight, False)

    for c in range(chunks):
        sent[c].wait_recv()
        forward([c], other)
    middle()
    backward_z()
    label_copy.wait_recv()
    weight = occupation(label_other[0:1, :], orbital_count)
    passed = []
    for c in range(chunks):
        backward_x(c, other, weight, True)
        for k, peer in enumerate(peers):
            give[k, :, columns(c)] = field[pl.ds(pl.multiple_of(peer * rows, rows), rows), columns(c)].astype(jnp.bfloat16)
            copy = pltpu.make_async_remote_copy(
                src_ref=give.at[k, :, columns(c)], dst_ref=take.at[k, :, columns(c)],
                send_sem=give_sem.at[k, c], recv_sem=take_sem.at[k, c],
                device_id={"group": peer}, device_id_type=mesh_id)
            copy.start()
            passed.append((c, k, copy))
    for c in range(chunks):
        total = field[pl.ds(pl.multiple_of(group * rows, rows), rows), columns(c)]
        for at, k, copy in passed:
            if at == c:
                copy.wait_recv()
                total = total + take[k, :, columns(c)].astype(jnp.float32)
        out_ref[0, :, columns(c)] = -total
    for _, _, copy in passed:
        copy.wait_send()
    for copy in sent:
        copy.wait_send()
    label_copy.wait_send()


def shards(trial, orbitals, labels, kernel_mask):
    n = trial.shape[1]
    bands, groups = lax.axis_size("band"), lax.axis_size("group")
    rows = n // groups
    chunks = n // (STACK * STACK)
    peers = groups - 1
    vmem = pl.BlockSpec(memory_space=pltpu.VMEM)
    hbm = pl.BlockSpec(memory_space=pltpu.HBM)
    dma = pltpu.SemaphoreType.DMA
    return pl.pallas_call(
        functools.partial(exchange_kernel, n, bands, groups),
        out_shape=jax.ShapeDtypeStruct((1, rows, n * n), jnp.float32),
        in_specs=[hbm, hbm, pl.BlockSpec(memory_space=pltpu.SMEM), hbm, hbm],
        out_specs=vmem,
        scratch_shapes=[
            pltpu.VMEM((STACK * n, STACK * n), jnp.bfloat16),
            pltpu.VMEM((n, n * n), jnp.bfloat16),
            pltpu.VMEM((n, n * n), jnp.bfloat16),
            pltpu.VMEM((n, n * n), jnp.bfloat16),
            pltpu.VMEM((n, n * n), jnp.int32),
            pltpu.VMEM((n * n // STACK, STACK * n), jnp.bfloat16),
            pltpu.VMEM((n * n // STACK, STACK * n), jnp.bfloat16),
            pltpu.VMEM((n // 2 * (n + PAD), 2 * n), jnp.float32),
            pltpu.VMEM((n // 2 * (n + PAD), 2 * n), jnp.float32),
            pltpu.VMEM((n // 2 * (n + PAD), 2 * n), jnp.float32),
            pltpu.VMEM((n, n * n), jnp.float32),
            pltpu.VMEM((8, STACK * n), jnp.int32),
            pltpu.VMEM((8, STACK * n), jnp.int32),
            pltpu.VMEM((peers, rows, n * n), jnp.bfloat16),
            pltpu.VMEM((peers, rows, n * n), jnp.bfloat16),
            dma((4,)), dma((chunks,)), dma((chunks,)), dma, dma, dma((peers, chunks)), dma((peers, chunks)),
        ],
        compiler_params=pltpu.CompilerParams(
            collective_id=0, has_side_effects=True, vmem_limit_bytes=63 * 1024 * 1024),
        name="exchange",
    )(trial, orbitals, labels, kernel_mask, cas_blocks(n))


def solution(mesh):
    in_specs = (P("band", None, None), P(("band", "group"), None, None), P(("band", "group")), P())
    out_specs = P("band", "group", None)
    return jax.shard_map(shards, mesh=mesh, in_specs=in_specs, out_specs=out_specs, check_vma=False)
```

```python
import functools

import jax
import jax.numpy as jnp
import ml_dtypes
import numpy as np
from jax import lax
from jax.experimental import pallas as pl
from jax.experimental.pallas import tpu as pltpu
from jax.sharding import PartitionSpec as P

screen_square = 16.0

STACK = 4
PAD = 1


def cas_blocks(grid_size):
    frequency = np.arange(grid_size)
    angle = (np.outer(frequency, frequency) % grid_size) * (2.0 * np.pi / grid_size)
    table = (np.cos(angle) + np.sin(angle)) / np.sqrt(grid_size)
    blocks = np.kron(np.eye(STACK), table).astype(np.float32)
    return jnp.asarray(blocks.astype(ml_dtypes.bfloat16))


def occupation(label_values, orbital_count):
    shifted = (label_values.astype(jnp.float32) - orbital_count / 2.0) / (orbital_count / 4.0)
    return 1.0 / (1.0 + jnp.exp(shifted))


def signed_square(index, grid_size):
    signed = jnp.where(index < grid_size // 2, index, index - grid_size)
    return (signed * signed).astype(jnp.float32)


def exchange_kernel(
    n, bands, groups,
    trial_hbm, orbital_hbm, label_ref, mask_hbm, blocks_hbm, out_hbm,
    table, result_part, target, own, other, mask, staged, back, cube, filtered, coulomb, field, label_own, label_other,
    give, take, local_sem, send_sem, recv_sem, label_send, label_recv, give_sem, take_sem, out_sem,
):
    band, group = lax.axis_index("band"), lax.axis_index("group")
    before = lax.rem(band + bands - 1, bands)
    after = lax.rem(band + 1, bands)
    half, lanes, wide = n // 2, 2 * n, STACK * n
    chunk = STACK * wide
    chunks = n * n // chunk
    planes = chunk // n
    pitch = n + PAD
    rows = n // groups
    mesh_id = pl.DeviceIdType.MESH

    def columns(c):
        return pl.ds(c * chunk, chunk)

    local = [
        pltpu.make_async_copy(orbital_hbm.at[0], own, local_sem.at[0]),
        pltpu.make_async_copy(trial_hbm.at[0], target, local_sem.at[1]),
        pltpu.make_async_copy(mask_hbm, mask, local_sem.at[2]),
        pltpu.make_async_copy(blocks_hbm, table, local_sem.at[3]),
    ]
    for at in (2, 0, 1, 3):
        local[at].start()
    label_own[...] = jnp.full(label_own.shape, label_ref[0], jnp.int32)

    barrier = pltpu.get_barrier_semaphore()
    peers = [lax.rem(group + k, groups) for k in range(1, groups)]
    for neighbour in (before, after):
        pl.semaphore_signal(barrier, inc=1, device_id={"band": neighbour}, device_id_type=mesh_id)
    for peer in peers:
        pl.semaphore_signal(barrier, inc=1, device_id={"group": peer}, device_id_type=mesh_id)
    pl.semaphore_wait(barrier, 2 + len(peers))

    sent = []
    for c in range(chunks):
        sent.append(pltpu.make_async_remote_copy(
            src_ref=orbital_hbm.at[0, :, columns(c)], dst_ref=other.at[:, columns(c)],
            send_sem=send_sem.at[c], recv_sem=recv_sem.at[c],
            device_id={"band": before}, device_id_type=mesh_id))
        sent[-1].start()
    label_copy = pltpu.make_async_remote_copy(
        src_ref=label_own, dst_ref=label_other, send_sem=label_send, recv_sem=label_recv,
        device_id={"band": before}, device_id_type=mesh_id)
    label_copy.start()

    left = lax.broadcasted_iota(jnp.int32, (half, lanes), 1) < n

    def matmul(a, b):
        return jnp.dot(a, b, preferred_element_type=jnp.float32)

    def exchanged(value):
        low, high = value[:half], value[half:]
        first = jnp.where(left, low, pltpu.roll(high, n, 1))
        second = jnp.where(left, pltpu.roll(low, n, 1), high)
        return first, second

    def restored(first, second):
        low = jnp.where(left, first, pltpu.roll(second, n, 1))
        high = jnp.where(left, pltpu.roll(first, n, 1), second)
        return jnp.concatenate([low, high], axis=0)

    def put_planes(ref, plane, value):
        for step, part in enumerate(exchanged(value)):
            ref[pl.ds(plane + step, half, stride=pitch), :] = part

    def forward(group_of_chunks, source):
        density = []
        for c in group_of_chunks:
            pieces = []
            for q in range(STACK):
                place = pl.ds(c * chunk + q * wide, wide)
                pieces.append(target[:, place] * source[:, place])
            density.append(jnp.concatenate(pieces, axis=0))
        first = matmul(blocks, jnp.concatenate(density, axis=1)).astype(jnp.bfloat16)
        for step, c in enumerate(group_of_chunks):
            staged[pl.ds(c * wide, wide), :] = first[:, step * wide:(step + 1) * wide]
        begin, count = group_of_chunks[0], len(group_of_chunks)
        second = matmul(staged[pl.ds(begin * wide, count * wide), :], blocks)
        for q in range(count * STACK):
            for h in range(wide // lanes):
                put_planes(cube, begin * planes + q * STACK + 2 * h,
                           second[q * n:(q + 1) * n, h * lanes:(h + 1) * lanes])

    def middle():
        sides = range(half // STACK)

        def gathered(ref):
            return jnp.concatenate([
                jnp.concatenate([
                    ref[pl.ds((side * STACK + q) * pitch, n), :] for q in range(STACK)
                ], axis=0) for side in sides
            ], axis=1)

        spectrum = matmul(blocks, gathered(cube).astype(jnp.bfloat16)) * gathered(coulomb)
        result = matmul(blocks, spectrum.astype(jnp.bfloat16))
        for side in sides:
            for q in range(STACK):
                filtered[pl.ds((side * STACK + q) * pitch, n), :] = (
                    result[q * n:(q + 1) * n, side * lanes:(side + 1) * lanes])

    def backward_z():
        for c in range(chunks):
            for q in range(STACK):
                for h in range(wide // lanes):
                    plane = c * planes + q * STACK + 2 * h
                    pair = restored(filtered[pl.ds(plane, half, stride=pitch), :],
                                    filtered[pl.ds(plane + 1, half, stride=pitch), :])
                    staged[pl.ds(c * wide + q * n, n), pl.ds(h * lanes, lanes)] = pair.astype(jnp.bfloat16)
        back[...] = matmul(staged[...], blocks).astype(jnp.bfloat16)

    def backward_x(group_of_chunks, source, weight, accumulate):
        operand = jnp.concatenate([back[pl.ds(c * wide, wide), :] for c in group_of_chunks], axis=1)
        potential = matmul(blocks, operand)
        for step, c in enumerate(group_of_chunks):
            for q in range(STACK):
                place = pl.ds(c * chunk + q * wide, wide)
                piece = potential[q * n:(q + 1) * n, step * wide:(step + 1) * wide]
                part = weight * piece * source[:, place].astype(jnp.float32)
                field[:, place] = field[:, place] + part if accumulate else part

    local[2].wait()
    ky_lane = lax.broadcasted_iota(jnp.int32, (n, lanes), 1)
    kx_row = lax.broadcasted_iota(jnp.int32, (n, lanes), 0)
    base = signed_square(kx_row, n) + signed_square(lax.rem(ky_lane, n), n) + screen_square
    for t in range(n // 2):
        ky = 2 * t + jnp.where(ky_lane < n, 0, 1)
        kept = mask[:, pl.ds(t * lanes, lanes)].astype(jnp.float32)
        put_planes(coulomb, 2 * t, kept * (screen_square / (base + signed_square(ky, n))))

    local[0].wait()
    local[1].wait()
    local[3].wait()
    blocks = table[...]
    orbital_count = bands * groups
    forward(range(chunks), own)
    middle()
    backward_z()
    weight = occupation(label_own[0:1, :], orbital_count)
    backward_x(range(chunks), own, weight, False)

    for c in range(chunks):
        sent[c].wait_recv()
        forward([c], other)
    middle()
    backward_z()
    label_copy.wait_recv()
    weight = occupation(label_other[0:1, :], orbital_count)
    passed = []
    for c in range(chunks):
        if c % 2 == 0:
            backward_x(range(c, min(c + 2, chunks)), other, weight, True)
        for k, peer in enumerate(peers):
            give[k, :, columns(c)] = field[pl.ds(pl.multiple_of(peer * rows, rows), rows), columns(c)].astype(jnp.bfloat16)
            copy = pltpu.make_async_remote_copy(
                src_ref=give.at[k, :, columns(c)], dst_ref=take.at[k, :, columns(c)],
                send_sem=give_sem.at[k, c], recv_sem=take_sem.at[k, c],
                device_id={"group": peer}, device_id_type=mesh_id)
            copy.start()
            passed.append((c, k, copy))
    finished = []
    for c in range(chunks):
        total = field[pl.ds(pl.multiple_of(group * rows, rows), rows), columns(c)]
        for at, k, copy in passed:
            if at == c:
                copy.wait_recv()
                total = total + take[k, :, columns(c)].astype(jnp.float32)
        result_part[:, columns(c)] = -total
        finished.append(pltpu.make_async_copy(
            result_part.at[:, columns(c)], out_hbm.at[0, :, columns(c)], out_sem.at[c]))
        finished[-1].start()
    for _, _, copy in passed:
        copy.wait_send()
    for copy in sent:
        copy.wait_send()
    label_copy.wait_send()
    for copy in finished:
        copy.wait()


def shards(trial, orbitals, labels, kernel_mask):
    n = trial.shape[1]
    bands, groups = lax.axis_size("band"), lax.axis_size("group")
    rows = n // groups
    chunks = n // (STACK * STACK)
    peers = groups - 1
    hbm = pl.BlockSpec(memory_space=pltpu.HBM)
    dma = pltpu.SemaphoreType.DMA
    return pl.pallas_call(
        functools.partial(exchange_kernel, n, bands, groups),
        out_shape=jax.ShapeDtypeStruct((1, rows, n * n), jnp.float32),
        in_specs=[hbm, hbm, pl.BlockSpec(memory_space=pltpu.SMEM), hbm, hbm],
        out_specs=hbm,
        scratch_shapes=[
            pltpu.VMEM((STACK * n, STACK * n), jnp.bfloat16),
            pltpu.VMEM((rows, n * n), jnp.float32),
            pltpu.VMEM((n, n * n), jnp.bfloat16),
            pltpu.VMEM((n, n * n), jnp.bfloat16),
            pltpu.VMEM((n, n * n), jnp.bfloat16),
            pltpu.VMEM((n, n * n), jnp.int32),
            pltpu.VMEM((n * n // STACK, STACK * n), jnp.bfloat16),
            pltpu.VMEM((n * n // STACK, STACK * n), jnp.bfloat16),
            pltpu.VMEM((n // 2 * (n + PAD), 2 * n), jnp.float32),
            pltpu.VMEM((n // 2 * (n + PAD), 2 * n), jnp.float32),
            pltpu.VMEM((n // 2 * (n + PAD), 2 * n), jnp.float32),
            pltpu.VMEM((n, n * n), jnp.float32),
            pltpu.VMEM((8, STACK * n), jnp.int32),
            pltpu.VMEM((8, STACK * n), jnp.int32),
            pltpu.VMEM((peers, rows, n * n), jnp.bfloat16),
            pltpu.VMEM((peers, rows, n * n), jnp.bfloat16),
            dma((4,)), dma((chunks,)), dma((chunks,)), dma, dma, dma((peers, chunks)), dma((peers, chunks)),
            dma((chunks,)),
        ],
        compiler_params=pltpu.CompilerParams(
            collective_id=0, has_side_effects=True, vmem_limit_bytes=63 * 1024 * 1024),
        name="exchange",
    )(trial, orbitals, labels, kernel_mask, cas_blocks(n))


def solution(mesh):
    in_specs = (P("band", None, None), P(("band", "group"), None, None), P(("band", "group")), P())
    out_specs = P("band", "group", None)
    return jax.shard_map(shards, mesh=mesh, in_specs=in_specs, out_specs=out_specs, check_vma=False)
```

```python
import functools

import jax
import jax.numpy as jnp
import ml_dtypes
import numpy as np
from jax import lax
from jax.experimental import pallas as pl
from jax.experimental.pallas import tpu as pltpu
from jax.sharding import PartitionSpec as P

screen_square = 16.0

STACK = 4
PAD = 1


def cas_blocks(grid_size):
    frequency = np.arange(grid_size)
    angle = (np.outer(frequency, frequency) % grid_size) * (2.0 * np.pi / grid_size)
    table = (np.cos(angle) + np.sin(angle)) / np.sqrt(grid_size)
    blocks = np.kron(np.eye(STACK), table).astype(np.float32)
    return jnp.asarray(blocks.astype(ml_dtypes.bfloat16))


def occupation(label_values, orbital_count):
    shifted = (label_values.astype(jnp.float32) - orbital_count / 2.0) / (orbital_count / 4.0)
    return 1.0 / (1.0 + jnp.exp(shifted))


def signed_square(index, grid_size):
    signed = jnp.where(index < grid_size // 2, index, index - grid_size)
    return (signed * signed).astype(jnp.float32)


def exchange_kernel(
    n, bands, groups,
    trial_hbm, orbital_hbm, label_ref, mask_hbm, blocks_hbm, out_hbm,
    table, result_part, target, own, other, mask, staged, back, cube, filtered, coulomb, field, label_own, label_other,
    give, take, local_sem, send_sem, recv_sem, label_send, label_recv, give_sem, take_sem, out_sem,
):
    band, group = lax.axis_index("band"), lax.axis_index("group")
    before = lax.rem(band + bands - 1, bands)
    after = lax.rem(band + 1, bands)
    half, lanes, wide = n // 2, 2 * n, STACK * n
    chunk = STACK * wide
    chunks = n * n // chunk
    planes = chunk // n
    pitch = n + PAD
    rows = n // groups
    mesh_id = pl.DeviceIdType.MESH

    def columns(c):
        return pl.ds(c * chunk, chunk)

    local = [
        pltpu.make_async_copy(orbital_hbm.at[0], own, local_sem.at[0]),
        pltpu.make_async_copy(trial_hbm.at[0], target, local_sem.at[1]),
        pltpu.make_async_copy(mask_hbm, mask, local_sem.at[2]),
        pltpu.make_async_copy(blocks_hbm, table, local_sem.at[3]),
    ]
    for at in (2, 0, 1, 3):
        local[at].start()
    label_own[...] = jnp.full(label_own.shape, label_ref[0], jnp.int32)

    barrier = pltpu.get_barrier_semaphore()
    peers = [lax.rem(group + k, groups) for k in range(1, groups)]
    for neighbour in (before, after):
        pl.semaphore_signal(barrier, inc=1, device_id={"band": neighbour}, device_id_type=mesh_id)
    for peer in peers:
        pl.semaphore_signal(barrier, inc=1, device_id={"group": peer}, device_id_type=mesh_id)
    pl.semaphore_wait(barrier, 2 + len(peers))

    sent = []
    for c in range(chunks):
        sent.append(pltpu.make_async_remote_copy(
            src_ref=orbital_hbm.at[0, :, columns(c)], dst_ref=other.at[:, columns(c)],
            send_sem=send_sem.at[c], recv_sem=recv_sem.at[c],
            device_id={"band": before}, device_id_type=mesh_id))
        sent[-1].start()
    label_copy = pltpu.make_async_remote_copy(
        src_ref=label_own, dst_ref=label_other, send_sem=label_send, recv_sem=label_recv,
        device_id={"band": before}, device_id_type=mesh_id)
    label_copy.start()

    left = lax.broadcasted_iota(jnp.int32, (half, lanes), 1) < n

    def matmul(a, b):
        return jnp.dot(a, b, preferred_element_type=jnp.float32)

    def exchanged(value):
        low, high = value[:half], value[half:]
        first = jnp.where(left, low, pltpu.roll(high, n, 1))
        second = jnp.where(left, pltpu.roll(low, n, 1), high)
        return first, second

    def restored(first, second):
        low = jnp.where(left, first, pltpu.roll(second, n, 1))
        high = jnp.where(left, pltpu.roll(first, n, 1), second)
        return jnp.concatenate([low, high], axis=0)

    def put_planes(ref, plane, value):
        for step, part in enumerate(exchanged(value)):
            ref[pl.ds(plane + step, half, stride=pitch), :] = part

    def forward(group_of_chunks, source):
        density = []
        for c in group_of_chunks:
            pieces = []
            for q in range(STACK):
                place = pl.ds(c * chunk + q * wide, wide)
                pieces.append(target[:, place] * source[:, place])
            density.append(jnp.concatenate(pieces, axis=0))
        first = matmul(blocks, jnp.concatenate(density, axis=1)).astype(jnp.bfloat16)
        for step, c in enumerate(group_of_chunks):
            staged[pl.ds(c * wide, wide), :] = first[:, step * wide:(step + 1) * wide]
        begin, count = group_of_chunks[0], len(group_of_chunks)
        second = matmul(staged[pl.ds(begin * wide, count * wide), :], blocks)
        for q in range(count * STACK):
            for h in range(wide // lanes):
                put_planes(cube, begin * planes + q * STACK + 2 * h,
                           second[q * n:(q + 1) * n, h * lanes:(h + 1) * lanes])

    def middle():
        sides = range(half // STACK)

        def gathered(ref):
            return jnp.concatenate([
                jnp.concatenate([
                    ref[pl.ds((side * STACK + q) * pitch, n), :] for q in range(STACK)
                ], axis=0) for side in sides
            ], axis=1)

        spectrum = matmul(blocks, gathered(cube).astype(jnp.bfloat16)) * gathered(coulomb)
        result = matmul(blocks, spectrum.astype(jnp.bfloat16))
        for side in sides:
            for q in range(STACK):
                filtered[pl.ds((side * STACK + q) * pitch, n), :] = (
                    result[q * n:(q + 1) * n, side * lanes:(side + 1) * lanes])

    def backward_z():
        for c in range(chunks):
            for q in range(STACK):
                for h in range(wide // lanes):
                    plane = c * planes + q * STACK + 2 * h
                    pair = restored(filtered[pl.ds(plane, half, stride=pitch), :],
                                    filtered[pl.ds(plane + 1, half, stride=pitch), :])
                    staged[pl.ds(c * wide + q * n, n), pl.ds(h * lanes, lanes)] = pair.astype(jnp.bfloat16)
        back[...] = matmul(staged[...], blocks).astype(jnp.bfloat16)

    def backward_x(group_of_chunks, source, weight, accumulate):
        operand = jnp.concatenate([back[pl.ds(c * wide, wide), :] for c in group_of_chunks], axis=1)
        potential = matmul(blocks, operand)
        for step, c in enumerate(group_of_chunks):
            for q in range(STACK):
                place = pl.ds(c * chunk + q * wide, wide)
                piece = potential[q * n:(q + 1) * n, step * wide:(step + 1) * wide]
                part = weight * piece * source[:, place].astype(jnp.float32)
                field[:, place] = field[:, place] + part if accumulate else part

    local[2].wait()
    ky_lane = lax.broadcasted_iota(jnp.int32, (n, lanes), 1)
    kx_row = lax.broadcasted_iota(jnp.int32, (n, lanes), 0)
    base = signed_square(kx_row, n) + signed_square(lax.rem(ky_lane, n), n) + screen_square
    for t in range(n // 2):
        ky = 2 * t + jnp.where(ky_lane < n, 0, 1)
        kept = mask[:, pl.ds(t * lanes, lanes)].astype(jnp.float32)
        put_planes(coulomb, 2 * t, kept * (screen_square / (base + signed_square(ky, n))))

    local[0].wait()
    local[1].wait()
    local[3].wait()
    blocks = table[...]
    orbital_count = bands * groups
    forward(range(chunks), own)
    middle()
    backward_z()
    weight = occupation(label_own[0:1, :], orbital_count)
    backward_x(range(chunks), own, weight, False)

    for c in range(chunks):
        sent[c].wait_recv()
        forward([c], other)
    middle()
    backward_z()
    label_copy.wait_recv()
    weight = occupation(label_other[0:1, :], orbital_count)
    passed = []
    for c in range(chunks):
        if c % 2 == 0:
            backward_x(range(c, min(c + 2, chunks)), other, weight, True)
        for k, peer in enumerate(peers):
            give[k, :, columns(c)] = field[pl.ds(pl.multiple_of(peer * rows, rows), rows), columns(c)].astype(jnp.bfloat16)
            copy = pltpu.make_async_remote_copy(
                src_ref=give.at[k, :, columns(c)], dst_ref=take.at[k, :, columns(c)],
                send_sem=give_sem.at[k, c], recv_sem=take_sem.at[k, c],
                device_id={"group": peer}, device_id_type=mesh_id)
            copy.start()
            passed.append((c, k, copy))
    finished = []
    for c in range(chunks):
        total = field[pl.ds(pl.multiple_of(group * rows, rows), rows), columns(c)]
        for at, k, copy in passed:
            if at == c:
                copy.wait_recv()
                total = total + take[k, :, columns(c)].astype(jnp.float32)
        result_part[:, columns(c)] = -total
        finished.append(pltpu.make_async_copy(
            result_part.at[:, columns(c)], out_hbm.at[0, :, columns(c)], out_sem.at[c]))
        finished[-1].start()
    for _, _, copy in passed:
        copy.wait_send()
    for copy in sent:
        copy.wait_send()
    label_copy.wait_send()
    for copy in finished:
        copy.wait()


def shards(trial, orbitals, labels, kernel_mask):
    n = trial.shape[1]
    bands, groups = lax.axis_size("band"), lax.axis_size("group")
    rows = n // groups
    chunks = n // (STACK * STACK)
    peers = groups - 1
    hbm = pl.BlockSpec(memory_space=pltpu.HBM)
    dma = pltpu.SemaphoreType.DMA
    return pl.pallas_call(
        functools.partial(exchange_kernel, n, bands, groups),
        out_shape=jax.ShapeDtypeStruct((1, rows, n * n), jnp.float32),
        in_specs=[hbm, hbm, pl.BlockSpec(memory_space=pltpu.SMEM), hbm, hbm],
        out_specs=hbm,
        scratch_shapes=[
            pltpu.VMEM((STACK * n, STACK * n), jnp.bfloat16),
            pltpu.VMEM((rows, n * n), jnp.float32),
            pltpu.VMEM((n, n * n), jnp.bfloat16),
            pltpu.VMEM((n, n * n), jnp.bfloat16),
            pltpu.VMEM((n, n * n), jnp.bfloat16),
            pltpu.VMEM((n, n * n), jnp.int32),
            pltpu.VMEM((n * n // STACK, STACK * n), jnp.bfloat16),
            pltpu.VMEM((n * n // STACK, STACK * n), jnp.bfloat16),
            pltpu.VMEM((n // 2 * (n + PAD), 2 * n), jnp.float32),
            pltpu.VMEM((n // 2 * (n + PAD), 2 * n), jnp.float32),
            pltpu.VMEM((n // 2 * (n + PAD), 2 * n), jnp.float32),
            pltpu.VMEM((n, n * n), jnp.float32),
            pltpu.VMEM((8, STACK * n), jnp.int32),
            pltpu.VMEM((8, STACK * n), jnp.int32),
            pltpu.VMEM((peers, rows, n * n), jnp.bfloat16),
            pltpu.VMEM((peers, rows, n * n), jnp.bfloat16),
            dma((4,)), dma((chunks,)), dma((chunks,)), dma, dma, dma((peers, chunks)), dma((peers, chunks)),
            dma((chunks,)),
        ],
        compiler_params=pltpu.CompilerParams(
            collective_id=0, has_side_effects=True, vmem_limit_bytes=53 * 1024 * 1024),
        name="exchange",
    )(trial, orbitals, labels, kernel_mask, cas_blocks(n))


def solution(mesh):
    in_specs = (P("band", None, None), P(("band", "group"), None, None), P(("band", "group")), P())
    out_specs = P("band", "group", None)
    return jax.shard_map(shards, mesh=mesh, in_specs=in_specs, out_specs=out_specs, check_vma=False)
```

```python
import functools

import jax
import jax.numpy as jnp
import ml_dtypes
import numpy as np
from jax import lax
from jax.experimental import pallas as pl
from jax.experimental.pallas import tpu as pltpu
from jax.sharding import PartitionSpec as P

screen_square = 16.0

STACK = 4
PAD = 1


def cas_blocks(grid_size):
    frequency = np.arange(grid_size)
    angle = (np.outer(frequency, frequency) % grid_size) * (2.0 * np.pi / grid_size)
    table = (np.cos(angle) + np.sin(angle)) / np.sqrt(grid_size)
    blocks = np.kron(np.eye(STACK), table).astype(np.float32)
    return jnp.asarray(blocks.astype(ml_dtypes.bfloat16))


def occupation(label_values, orbital_count):
    shifted = (label_values.astype(jnp.float32) - orbital_count / 2.0) / (orbital_count / 4.0)
    return 1.0 / (1.0 + jnp.exp(shifted))


def signed_square(index, grid_size):
    signed = jnp.where(index < grid_size // 2, index, index - grid_size)
    return (signed * signed).astype(jnp.float32)


def exchange_kernel(
    n, bands, groups,
    trial_hbm, orbital_hbm, label_ref, mask_hbm, blocks_hbm, out_hbm,
    table, result_part, target, own, other, mask, staged, back, cube, filtered, coulomb, field, label_own, label_other,
    give, take, local_sem, send_sem, recv_sem, label_send, label_recv, give_sem, take_sem, out_sem,
):
    band, group = lax.axis_index("band"), lax.axis_index("group")
    before = lax.rem(band + bands - 1, bands)
    after = lax.rem(band + 1, bands)
    half, lanes, wide = n // 2, 2 * n, STACK * n
    chunk = STACK * wide
    chunks = n * n // chunk
    planes = chunk // n
    pitch = n + PAD
    rows = n // groups
    mesh_id = pl.DeviceIdType.MESH

    def columns(c):
        return pl.ds(c * chunk, chunk)

    local = [
        pltpu.make_async_copy(orbital_hbm.at[0], own, local_sem.at[0]),
        pltpu.make_async_copy(trial_hbm.at[0], target, local_sem.at[1]),
        pltpu.make_async_copy(mask_hbm, mask, local_sem.at[2]),
        pltpu.make_async_copy(blocks_hbm, table, local_sem.at[3]),
    ]
    for at in (2, 0, 1, 3):
        local[at].start()
    label_own[...] = jnp.full(label_own.shape, label_ref[0], jnp.int32)

    barrier = pltpu.get_barrier_semaphore()
    peers = [lax.rem(group + k, groups) for k in range(1, groups)]
    for neighbour in (before, after):
        pl.semaphore_signal(barrier, inc=1, device_id={"band": neighbour}, device_id_type=mesh_id)
    for peer in peers:
        pl.semaphore_signal(barrier, inc=1, device_id={"group": peer}, device_id_type=mesh_id)
    pl.semaphore_wait(barrier, 2 + len(peers))

    sent = []
    for c in range(chunks):
        sent.append(pltpu.make_async_remote_copy(
            src_ref=orbital_hbm.at[0, :, columns(c)], dst_ref=other.at[:, columns(c)],
            send_sem=send_sem.at[c], recv_sem=recv_sem.at[c],
            device_id={"band": before}, device_id_type=mesh_id))
    label_copy = pltpu.make_async_remote_copy(
        src_ref=label_own, dst_ref=label_other, send_sem=label_send, recv_sem=label_recv,
        device_id={"band": before}, device_id_type=mesh_id)
    label_copy.start()
    for copy in sent[:-1]:
        copy.start()

    left = lax.broadcasted_iota(jnp.int32, (half, lanes), 1) < n

    def matmul(a, b):
        return jnp.dot(a, b, preferred_element_type=jnp.float32)

    def exchanged(value):
        low, high = value[:half], value[half:]
        first = jnp.where(left, low, pltpu.roll(high, n, 1))
        second = jnp.where(left, pltpu.roll(low, n, 1), high)
        return first, second

    def restored(first, second):
        low = jnp.where(left, first, pltpu.roll(second, n, 1))
        high = jnp.where(left, pltpu.roll(first, n, 1), second)
        return jnp.concatenate([low, high], axis=0)

    def put_planes(ref, plane, value):
        for step, part in enumerate(exchanged(value)):
            ref[pl.ds(plane + step, half, stride=pitch), :] = part

    def forward(group_of_chunks, source):
        density = []
        for c in group_of_chunks:
            pieces = []
            for q in range(STACK):
                place = pl.ds(c * chunk + q * wide, wide)
                pieces.append(target[:, place] * source[:, place])
            density.append(jnp.concatenate(pieces, axis=0))
        first = matmul(blocks, jnp.concatenate(density, axis=1)).astype(jnp.bfloat16)
        for step, c in enumerate(group_of_chunks):
            staged[pl.ds(c * wide, wide), :] = first[:, step * wide:(step + 1) * wide]
        begin, count = group_of_chunks[0], len(group_of_chunks)
        second = matmul(staged[pl.ds(begin * wide, count * wide), :], blocks)
        for q in range(count * STACK):
            for h in range(wide // lanes):
                put_planes(cube, begin * planes + q * STACK + 2 * h,
                           second[q * n:(q + 1) * n, h * lanes:(h + 1) * lanes])

    def middle():
        sides = range(half // STACK)

        def gathered(ref):
            return jnp.concatenate([
                jnp.concatenate([
                    ref[pl.ds((side * STACK + q) * pitch, n), :] for q in range(STACK)
                ], axis=0) for side in sides
            ], axis=1)

        spectrum = matmul(blocks, gathered(cube).astype(jnp.bfloat16)) * gathered(coulomb)
        result = matmul(blocks, spectrum.astype(jnp.bfloat16))
        for side in sides:
            for q in range(STACK):
                filtered[pl.ds((side * STACK + q) * pitch, n), :] = (
                    result[q * n:(q + 1) * n, side * lanes:(side + 1) * lanes])

    def backward_z():
        for c in range(chunks):
            for q in range(STACK):
                for h in range(wide // lanes):
                    plane = c * planes + q * STACK + 2 * h
                    pair = restored(filtered[pl.ds(plane, half, stride=pitch), :],
                                    filtered[pl.ds(plane + 1, half, stride=pitch), :])
                    staged[pl.ds(c * wide + q * n, n), pl.ds(h * lanes, lanes)] = pair.astype(jnp.bfloat16)
        back[...] = matmul(staged[...], blocks).astype(jnp.bfloat16)

    def backward_x(group_of_chunks, source, weight, accumulate):
        operand = jnp.concatenate([back[pl.ds(c * wide, wide), :] for c in group_of_chunks], axis=1)
        potential = matmul(blocks, operand)
        for step, c in enumerate(group_of_chunks):
            for q in range(STACK):
                place = pl.ds(c * chunk + q * wide, wide)
                piece = potential[q * n:(q + 1) * n, step * wide:(step + 1) * wide]
                part = weight * piece * source[:, place].astype(jnp.float32)
                field[:, place] = field[:, place] + part if accumulate else part

    local[2].wait()
    ky_lane = lax.broadcasted_iota(jnp.int32, (n, lanes), 1)
    kx_row = lax.broadcasted_iota(jnp.int32, (n, lanes), 0)
    base = signed_square(kx_row, n) + signed_square(lax.rem(ky_lane, n), n) + screen_square
    for t in range(n // 2):
        ky = 2 * t + jnp.where(ky_lane < n, 0, 1)
        kept = mask[:, pl.ds(t * lanes, lanes)].astype(jnp.float32)
        put_planes(coulomb, 2 * t, kept * (screen_square / (base + signed_square(ky, n))))

    local[0].wait()
    local[1].wait()
    local[3].wait()
    blocks = table[...]
    orbital_count = bands * groups
    forward(range(chunks), own)
    middle()
    backward_z()
    weight = occupation(label_own[0:1, :], orbital_count)
    backward_x(range(chunks), own, weight, False)

    sent[0].wait_send()
    sent[-1].start()
    for c in range(chunks):
        sent[c].wait_recv()
        forward([c], other)
    middle()
    backward_z()
    label_copy.wait_recv()
    weight = occupation(label_other[0:1, :], orbital_count)
    passed = []
    for c in range(chunks):
        if c % 2 == 0:
            backward_x(range(c, min(c + 2, chunks)), other, weight, True)
        for k, peer in enumerate(peers):
            give[k, :, columns(c)] = field[pl.ds(pl.multiple_of(peer * rows, rows), rows), columns(c)].astype(jnp.bfloat16)
            copy = pltpu.make_async_remote_copy(
                src_ref=give.at[k, :, columns(c)], dst_ref=take.at[k, :, columns(c)],
                send_sem=give_sem.at[k, c], recv_sem=take_sem.at[k, c],
                device_id={"group": peer}, device_id_type=mesh_id)
            copy.start()
            passed.append((c, k, copy))
    finished = []
    for c in range(chunks):
        total = field[pl.ds(pl.multiple_of(group * rows, rows), rows), columns(c)]
        for at, k, copy in passed:
            if at == c:
                copy.wait_recv()
                total = total + take[k, :, columns(c)].astype(jnp.float32)
        result_part[:, columns(c)] = -total
        finished.append(pltpu.make_async_copy(
            result_part.at[:, columns(c)], out_hbm.at[0, :, columns(c)], out_sem.at[c]))
        finished[-1].start()
    for _, _, copy in passed:
        copy.wait_send()
    for copy in sent[1:]:
        copy.wait_send()
    label_copy.wait_send()
    for copy in finished:
        copy.wait()


def shards(trial, orbitals, labels, kernel_mask):
    n = trial.shape[1]
    bands, groups = lax.axis_size("band"), lax.axis_size("group")
    rows = n // groups
    chunks = n // (STACK * STACK)
    peers = groups - 1
    hbm = pl.BlockSpec(memory_space=pltpu.HBM)
    dma = pltpu.SemaphoreType.DMA
    return pl.pallas_call(
        functools.partial(exchange_kernel, n, bands, groups),
        out_shape=jax.ShapeDtypeStruct((1, rows, n * n), jnp.float32),
        in_specs=[hbm, hbm, pl.BlockSpec(memory_space=pltpu.SMEM), hbm, hbm],
        out_specs=hbm,
        scratch_shapes=[
            pltpu.VMEM((STACK * n, STACK * n), jnp.bfloat16),
            pltpu.VMEM((rows, n * n), jnp.float32),
            pltpu.VMEM((n, n * n), jnp.bfloat16),
            pltpu.VMEM((n, n * n), jnp.bfloat16),
            pltpu.VMEM((n, n * n), jnp.bfloat16),
            pltpu.VMEM((n, n * n), jnp.int32),
            pltpu.VMEM((n * n // STACK, STACK * n), jnp.bfloat16),
            pltpu.VMEM((n * n // STACK, STACK * n), jnp.bfloat16),
            pltpu.VMEM((n // 2 * (n + PAD), 2 * n), jnp.float32),
            pltpu.VMEM((n // 2 * (n + PAD), 2 * n), jnp.float32),
            pltpu.VMEM((n // 2 * (n + PAD), 2 * n), jnp.float32),
            pltpu.VMEM((n, n * n), jnp.float32),
            pltpu.VMEM((8, STACK * n), jnp.int32),
            pltpu.VMEM((8, STACK * n), jnp.int32),
            pltpu.VMEM((peers, rows, n * n), jnp.bfloat16),
            pltpu.VMEM((peers, rows, n * n), jnp.bfloat16),
            dma((4,)), dma((chunks,)), dma((chunks,)), dma, dma, dma((peers, chunks)), dma((peers, chunks)),
            dma((chunks,)),
        ],
        compiler_params=pltpu.CompilerParams(
            collective_id=0, has_side_effects=True, vmem_limit_bytes=53 * 1024 * 1024),
        name="exchange",
    )(trial, orbitals, labels, kernel_mask, cas_blocks(n))


def solution(mesh):
    in_specs = (P("band", None, None), P(("band", "group"), None, None), P(("band", "group")), P())
    out_specs = P("band", "group", None)
    return jax.shard_map(shards, mesh=mesh, in_specs=in_specs, out_specs=out_specs, check_vma=False)
```

```python
import functools

import jax
import jax.numpy as jnp
import numpy as np
from jax import lax
from jax.experimental import pallas as pl
from jax.experimental.pallas import tpu as pltpu
from jax.sharding import PartitionSpec as P

screen_square = 16.0

STACK = 4
PAD = 1


def cas_blocks(grid_size):
    shape = (grid_size, 2 * grid_size)
    row = lax.broadcasted_iota(jnp.int32, shape, 0)
    column = lax.rem(lax.broadcasted_iota(jnp.int32, shape, 1), grid_size)
    angle = lax.rem(row * column, grid_size).astype(jnp.float32) * (2.0 * np.pi / grid_size)
    table = (jnp.cos(angle) + jnp.sin(angle)) * np.float32(1.0 / np.sqrt(grid_size))
    table = jnp.concatenate([table] * (STACK // 2), axis=1)
    owner = lax.broadcasted_iota(jnp.int32, table.shape, 1) // grid_size
    blocks = [jnp.where(owner == block, table, 0.0) for block in range(STACK)]
    return jnp.concatenate(blocks, axis=0).astype(jnp.bfloat16)


def occupation(label_values, orbital_count):
    shifted = (label_values.astype(jnp.float32) - orbital_count / 2.0) / (orbital_count / 4.0)
    return 1.0 / (1.0 + jnp.exp(shifted))


def signed_square(index, grid_size):
    signed = jnp.where(index < grid_size // 2, index, index - grid_size)
    return (signed * signed).astype(jnp.float32)


def exchange_kernel(
    n, bands, groups,
    trial_hbm, orbital_hbm, label_ref, mask_hbm, out_hbm,
    table, result_part, target, own, other, mask, staged, back, cube, filtered, coulomb, field, label_own, label_other,
    give, take, local_sem, send_sem, recv_sem, label_send, label_recv, give_sem, take_sem, out_sem,
):
    band, group = lax.axis_index("band"), lax.axis_index("group")
    before = lax.rem(band + bands - 1, bands)
    after = lax.rem(band + 1, bands)
    half, lanes, wide = n // 2, 2 * n, STACK * n
    chunk = STACK * wide
    chunks = n * n // chunk
    planes = chunk // n
    pitch = n + PAD
    rows = n // groups
    mesh_id = pl.DeviceIdType.MESH

    def columns(c):
        return pl.ds(c * chunk, chunk)

    local = [
        pltpu.make_async_copy(orbital_hbm.at[0], own, local_sem.at[0]),
        pltpu.make_async_copy(trial_hbm.at[0], target, local_sem.at[1]),
        pltpu.make_async_copy(mask_hbm, mask, local_sem.at[2]),
    ]
    for at in (2, 0, 1):
        local[at].start()
    label_own[...] = jnp.full(label_own.shape, label_ref[0], jnp.int32)

    barrier = pltpu.get_barrier_semaphore()
    peers = [lax.rem(group + k, groups) for k in range(1, groups)]
    for neighbour in (before, after):
        pl.semaphore_signal(barrier, inc=1, device_id={"band": neighbour}, device_id_type=mesh_id)
    for peer in peers:
        pl.semaphore_signal(barrier, inc=1, device_id={"group": peer}, device_id_type=mesh_id)
    pl.semaphore_wait(barrier, 2 + len(peers))

    sent = []
    for c in range(chunks):
        sent.append(pltpu.make_async_remote_copy(
            src_ref=orbital_hbm.at[0, :, columns(c)], dst_ref=other.at[:, columns(c)],
            send_sem=send_sem.at[c], recv_sem=recv_sem.at[c],
            device_id={"band": before}, device_id_type=mesh_id))
    label_copy = pltpu.make_async_remote_copy(
        src_ref=label_own, dst_ref=label_other, send_sem=label_send, recv_sem=label_recv,
        device_id={"band": before}, device_id_type=mesh_id)
    label_copy.start()
    for copy in sent[:-1]:
        copy.start()

    left = lax.broadcasted_iota(jnp.int32, (half, lanes), 1) < n

    def matmul(a, b):
        return jnp.dot(a, b, preferred_element_type=jnp.float32)

    def exchanged(value):
        low, high = value[:half], value[half:]
        first = jnp.where(left, low, pltpu.roll(high, n, 1))
        second = jnp.where(left, pltpu.roll(low, n, 1), high)
        return first, second

    def restored(first, second):
        low = jnp.where(left, first, pltpu.roll(second, n, 1))
        high = jnp.where(left, pltpu.roll(first, n, 1), second)
        return jnp.concatenate([low, high], axis=0)

    def put_planes(ref, plane, value):
        for step, part in enumerate(exchanged(value)):
            ref[pl.ds(plane + step, half, stride=pitch), :] = part

    def forward(group_of_chunks, source):
        density = []
        for c in group_of_chunks:
            pieces = []
            for q in range(STACK):
                place = pl.ds(c * chunk + q * wide, wide)
                pieces.append(target[:, place] * source[:, place])
            density.append(jnp.concatenate(pieces, axis=0))
        first = matmul(blocks, jnp.concatenate(density, axis=1)).astype(jnp.bfloat16)
        for step, c in enumerate(group_of_chunks):
            staged[pl.ds(c * wide, wide), :] = first[:, step * wide:(step + 1) * wide]
        begin, count = group_of_chunks[0], len(group_of_chunks)
        second = matmul(staged[pl.ds(begin * wide, count * wide), :], blocks)
        for q in range(count * STACK):
            for h in range(wide // lanes):
                put_planes(cube, begin * planes + q * STACK + 2 * h,
                           second[q * n:(q + 1) * n, h * lanes:(h + 1) * lanes])

    def middle():
        sides = range(half // STACK)

        def gathered(ref):
            return jnp.concatenate([
                jnp.concatenate([
                    ref[pl.ds((side * STACK + q) * pitch, n), :] for q in range(STACK)
                ], axis=0) for side in sides
            ], axis=1)

        spectrum = matmul(blocks, gathered(cube).astype(jnp.bfloat16)) * gathered(coulomb)
        result = matmul(blocks, spectrum.astype(jnp.bfloat16))
        for side in sides:
            for q in range(STACK):
                filtered[pl.ds((side * STACK + q) * pitch, n), :] = (
                    result[q * n:(q + 1) * n, side * lanes:(side + 1) * lanes])

    def backward_z():
        for c in range(chunks):
            for q in range(STACK):
                for h in range(wide // lanes):
                    plane = c * planes + q * STACK + 2 * h
                    pair = restored(filtered[pl.ds(plane, half, stride=pitch), :],
                                    filtered[pl.ds(plane + 1, half, stride=pitch), :])
                    staged[pl.ds(c * wide + q * n, n), pl.ds(h * lanes, lanes)] = pair.astype(jnp.bfloat16)
        back[...] = matmul(staged[...], blocks).astype(jnp.bfloat16)

    def backward_x(group_of_chunks, source, weight, accumulate):
        operand = jnp.concatenate([back[pl.ds(c * wide, wide), :] for c in group_of_chunks], axis=1)
        potential = matmul(blocks, operand)
        for step, c in enumerate(group_of_chunks):
            for q in range(STACK):
                place = pl.ds(c * chunk + q * wide, wide)
                piece = potential[q * n:(q + 1) * n, step * wide:(step + 1) * wide]
                part = weight * piece * source[:, place].astype(jnp.float32)
                field[:, place] = field[:, place] + part if accumulate else part

    table[...] = cas_blocks(n)
    local[2].wait()
    ky_lane = lax.broadcasted_iota(jnp.int32, (n, lanes), 1)
    kx_row = lax.broadcasted_iota(jnp.int32, (n, lanes), 0)
    base = signed_square(kx_row, n) + signed_square(lax.rem(ky_lane, n), n) + screen_square
    for t in range(n // 2):
        ky = 2 * t + jnp.where(ky_lane < n, 0, 1)
        kept = mask[:, pl.ds(t * lanes, lanes)].astype(jnp.float32)
        put_planes(coulomb, 2 * t, kept * (screen_square / (base + signed_square(ky, n))))

    local[0].wait()
    local[1].wait()
    blocks = table[...]
    orbital_count = bands * groups
    forward(range(chunks), own)
    middle()
    backward_z()
    weight = occupation(label_own[0:1, :], orbital_count)
    backward_x(range(chunks), own, weight, False)

    sent[0].wait_send()
    sent[-1].start()
    for c in range(chunks):
        sent[c].wait_recv()
        forward([c], other)
    middle()
    backward_z()
    label_copy.wait_recv()
    weight = occupation(label_other[0:1, :], orbital_count)
    passed = []
    for c in range(chunks):
        if c % 2 == 0:
            backward_x(range(c, min(c + 2, chunks)), other, weight, True)
        for k, peer in enumerate(peers):
            give[k, :, columns(c)] = field[pl.ds(pl.multiple_of(peer * rows, rows), rows), columns(c)].astype(jnp.bfloat16)
            copy = pltpu.make_async_remote_copy(
                src_ref=give.at[k, :, columns(c)], dst_ref=take.at[k, :, columns(c)],
                send_sem=give_sem.at[k, c], recv_sem=take_sem.at[k, c],
                device_id={"group": peer}, device_id_type=mesh_id)
            copy.start()
            passed.append((c, k, copy))
    finished = []
    for c in range(chunks):
        total = field[pl.ds(pl.multiple_of(group * rows, rows), rows), columns(c)]
        for at, k, copy in passed:
            if at == c:
                copy.wait_recv()
                total = total + take[k, :, columns(c)].astype(jnp.float32)
        result_part[:, columns(c)] = -total
        finished.append(pltpu.make_async_copy(
            result_part.at[:, columns(c)], out_hbm.at[0, :, columns(c)], out_sem.at[c]))
        finished[-1].start()
    for _, _, copy in passed:
        copy.wait_send()
    for copy in sent[1:]:
        copy.wait_send()
    label_copy.wait_send()
    for copy in finished:
        copy.wait()


def shards(trial, orbitals, labels, kernel_mask):
    n = trial.shape[1]
    bands, groups = lax.axis_size("band"), lax.axis_size("group")
    rows = n // groups
    chunks = n // (STACK * STACK)
    peers = groups - 1
    hbm = pl.BlockSpec(memory_space=pltpu.HBM)
    dma = pltpu.SemaphoreType.DMA
    return pl.pallas_call(
        functools.partial(exchange_kernel, n, bands, groups),
        out_shape=jax.ShapeDtypeStruct((1, rows, n * n), jnp.float32),
        in_specs=[hbm, hbm, pl.BlockSpec(memory_space=pltpu.SMEM), hbm],
        out_specs=hbm,
        scratch_shapes=[
            pltpu.VMEM((STACK * n, STACK * n), jnp.bfloat16),
            pltpu.VMEM((rows, n * n), jnp.float32),
            pltpu.VMEM((n, n * n), jnp.bfloat16),
            pltpu.VMEM((n, n * n), jnp.bfloat16),
            pltpu.VMEM((n, n * n), jnp.bfloat16),
            pltpu.VMEM((n, n * n), jnp.int32),
            pltpu.VMEM((n * n // STACK, STACK * n), jnp.bfloat16),
            pltpu.VMEM((n * n // STACK, STACK * n), jnp.bfloat16),
            pltpu.VMEM((n // 2 * (n + PAD), 2 * n), jnp.float32),
            pltpu.VMEM((n // 2 * (n + PAD), 2 * n), jnp.float32),
            pltpu.VMEM((n // 2 * (n + PAD), 2 * n), jnp.float32),
            pltpu.VMEM((n, n * n), jnp.float32),
            pltpu.VMEM((8, STACK * n), jnp.int32),
            pltpu.VMEM((8, STACK * n), jnp.int32),
            pltpu.VMEM((peers, rows, n * n), jnp.bfloat16),
            pltpu.VMEM((peers, rows, n * n), jnp.bfloat16),
            dma((3,)), dma((chunks,)), dma((chunks,)), dma, dma, dma((peers, chunks)), dma((peers, chunks)),
            dma((chunks,)),
        ],
        compiler_params=pltpu.CompilerParams(
            collective_id=0, has_side_effects=True, vmem_limit_bytes=53 * 1024 * 1024),
        name="exchange",
    )(trial, orbitals, labels, kernel_mask)


def solution(mesh):
    in_specs = (P("band", None, None), P(("band", "group"), None, None), P(("band", "group")), P())
    out_specs = P("band", "group", None)
    return jax.shard_map(shards, mesh=mesh, in_specs=in_specs, out_specs=out_specs, check_vma=False)
```

```python
import functools

import jax
import jax.numpy as jnp
import numpy as np
from jax import lax
from jax.experimental import pallas as pl
from jax.experimental.pallas import tpu as pltpu
from jax.sharding import PartitionSpec as P

screen_square = 16.0

STACK = 4
PAD = 1


def cas_blocks(grid_size):
    shape = (grid_size, 2 * grid_size)
    row = lax.broadcasted_iota(jnp.int32, shape, 0)
    column = lax.rem(lax.broadcasted_iota(jnp.int32, shape, 1), grid_size)
    angle = lax.rem(row * column, grid_size).astype(jnp.float32) * (2.0 * np.pi / grid_size)
    table = (jnp.cos(angle) + jnp.sin(angle)) * np.float32(1.0 / np.sqrt(grid_size))
    table = jnp.concatenate([table] * (STACK // 2), axis=1)
    owner = lax.broadcasted_iota(jnp.int32, table.shape, 1) // grid_size
    blocks = [jnp.where(owner == block, table, 0.0) for block in range(STACK)]
    return jnp.concatenate(blocks, axis=0).astype(jnp.bfloat16)


def occupation(label_values, orbital_count):
    shifted = (label_values.astype(jnp.float32) - orbital_count / 2.0) / (orbital_count / 4.0)
    return 1.0 / (1.0 + jnp.exp(shifted))


def signed_square(index, grid_size):
    signed = jnp.where(index < grid_size // 2, index, index - grid_size)
    return (signed * signed).astype(jnp.float32)


def exchange_kernel(
    n, bands, groups,
    trial_hbm, orbital_hbm, label_ref, mask_hbm, out_ref,
    table, target, own, other, mask, staged, back, cube, filtered, coulomb, field, label_own, label_other,
    give, take, local_sem, send_sem, recv_sem, label_send, label_recv, give_sem, take_sem,
):
    band, group = lax.axis_index("band"), lax.axis_index("group")
    before = lax.rem(band + bands - 1, bands)
    after = lax.rem(band + 1, bands)
    half, lanes, wide = n // 2, 2 * n, STACK * n
    chunk = STACK * wide
    chunks = n * n // chunk
    planes = chunk // n
    pitch = n + PAD
    rows = n // groups
    mesh_id = pl.DeviceIdType.MESH

    def columns(c):
        return pl.ds(c * chunk, chunk)

    barrier = pltpu.get_barrier_semaphore()
    peers = [lax.rem(group + k, groups) for k in range(1, groups)]
    for neighbour in (before, after):
        pl.semaphore_signal(barrier, inc=1, device_id={"band": neighbour}, device_id_type=mesh_id)
    for peer in peers:
        pl.semaphore_signal(barrier, inc=1, device_id={"group": peer}, device_id_type=mesh_id)
    local = [
        pltpu.make_async_copy(orbital_hbm.at[0], own, local_sem.at[0]),
        pltpu.make_async_copy(trial_hbm.at[0], target, local_sem.at[1]),
        pltpu.make_async_copy(mask_hbm, mask, local_sem.at[2]),
    ]
    for at in (2, 0, 1):
        local[at].start()
    label_own[...] = jnp.full(label_own.shape, label_ref[0], jnp.int32)

    pl.semaphore_wait(barrier, 2 + len(peers))

    sent = []
    for c in range(chunks):
        sent.append(pltpu.make_async_remote_copy(
            src_ref=orbital_hbm.at[0, :, columns(c)], dst_ref=other.at[:, columns(c)],
            send_sem=send_sem.at[c], recv_sem=recv_sem.at[c],
            device_id={"band": before}, device_id_type=mesh_id))
    label_copy = pltpu.make_async_remote_copy(
        src_ref=label_own, dst_ref=label_other, send_sem=label_send, recv_sem=label_recv,
        device_id={"band": before}, device_id_type=mesh_id)
    label_copy.start()
    for copy in sent[:-1]:
        copy.start()

    left = lax.broadcasted_iota(jnp.int32, (half, lanes), 1) < n

    def matmul(a, b):
        return jnp.dot(a, b, preferred_element_type=jnp.float32)

    def exchanged(value):
        low, high = value[:half], value[half:]
        first = jnp.where(left, low, pltpu.roll(high, n, 1))
        second = jnp.where(left, pltpu.roll(low, n, 1), high)
        return first, second

    def restored(first, second):
        low = jnp.where(left, first, pltpu.roll(second, n, 1))
        high = jnp.where(left, pltpu.roll(first, n, 1), second)
        return jnp.concatenate([low, high], axis=0)

    def put_planes(ref, plane, value):
        for step, part in enumerate(exchanged(value)):
            ref[pl.ds(plane + step, half, stride=pitch), :] = part

    def forward(group_of_chunks, source):
        density = []
        for c in group_of_chunks:
            pieces = []
            for q in range(STACK):
                place = pl.ds(c * chunk + q * wide, wide)
                pieces.append(target[:, place] * source[:, place])
            density.append(jnp.concatenate(pieces, axis=0))
        first = matmul(blocks, jnp.concatenate(density, axis=1)).astype(jnp.bfloat16)
        for step, c in enumerate(group_of_chunks):
            staged[pl.ds(c * wide, wide), :] = first[:, step * wide:(step + 1) * wide]
        begin, count = group_of_chunks[0], len(group_of_chunks)
        second = matmul(staged[pl.ds(begin * wide, count * wide), :], blocks)
        for q in range(count * STACK):
            for h in range(wide // lanes):
                put_planes(cube, begin * planes + q * STACK + 2 * h,
                           second[q * n:(q + 1) * n, h * lanes:(h + 1) * lanes])

    def middle():
        sides = range(half // STACK)

        def gathered(ref):
            return jnp.concatenate([
                jnp.concatenate([
                    ref[pl.ds((side * STACK + q) * pitch, n), :] for q in range(STACK)
                ], axis=0) for side in sides
            ], axis=1)

        spectrum = matmul(blocks, gathered(cube).astype(jnp.bfloat16)) * gathered(coulomb)
        result = matmul(blocks, spectrum.astype(jnp.bfloat16))
        for side in sides:
            for q in range(STACK):
                filtered[pl.ds((side * STACK + q) * pitch, n), :] = (
                    result[q * n:(q + 1) * n, side * lanes:(side + 1) * lanes])

    def backward_z():
        for c in range(chunks):
            for q in range(STACK):
                for h in range(wide // lanes):
                    plane = c * planes + q * STACK + 2 * h
                    pair = restored(filtered[pl.ds(plane, half, stride=pitch), :],
                                    filtered[pl.ds(plane + 1, half, stride=pitch), :])
                    staged[pl.ds(c * wide + q * n, n), pl.ds(h * lanes, lanes)] = pair.astype(jnp.bfloat16)
        back[...] = matmul(staged[...], blocks).astype(jnp.bfloat16)

    def backward_x(group_of_chunks, source, weight, accumulate):
        operand = jnp.concatenate([back[pl.ds(c * wide, wide), :] for c in group_of_chunks], axis=1)
        potential = matmul(blocks, operand)
        for step, c in enumerate(group_of_chunks):
            for q in range(STACK):
                place = pl.ds(c * chunk + q * wide, wide)
                piece = potential[q * n:(q + 1) * n, step * wide:(step + 1) * wide]
                part = weight * piece * source[:, place].astype(jnp.float32)
                field[:, place] = field[:, place] + part if accumulate else part

    table[...] = cas_blocks(n)
    local[2].wait()
    ky_lane = lax.broadcasted_iota(jnp.int32, (n, lanes), 1)
    kx_row = lax.broadcasted_iota(jnp.int32, (n, lanes), 0)
    base = signed_square(kx_row, n) + signed_square(lax.rem(ky_lane, n), n) + screen_square
    for t in range(n // 2):
        ky = 2 * t + jnp.where(ky_lane < n, 0, 1)
        kept = mask[:, pl.ds(t * lanes, lanes)].astype(jnp.float32)
        put_planes(coulomb, 2 * t, kept * (screen_square / (base + signed_square(ky, n))))

    local[0].wait()
    local[1].wait()
    blocks = table[...]
    orbital_count = bands * groups
    forward(range(chunks), own)
    middle()
    backward_z()
    weight = occupation(label_own[0:1, :], orbital_count)
    backward_x(range(chunks), own, weight, False)

    sent[0].wait_send()
    sent[-1].start()
    for c in range(chunks):
        sent[c].wait_recv()
        forward([c], other)
    middle()
    backward_z()
    label_copy.wait_recv()
    weight = occupation(label_other[0:1, :], orbital_count)
    passed = []
    for c in range(chunks):
        if c % 2 == 0:
            backward_x(range(c, min(c + 2, chunks)), other, weight, True)
        for k, peer in enumerate(peers):
            give[k, :, columns(c)] = field[pl.ds(pl.multiple_of(peer * rows, rows), rows), columns(c)].astype(jnp.bfloat16)
            copy = pltpu.make_async_remote_copy(
                src_ref=give.at[k, :, columns(c)], dst_ref=take.at[k, :, columns(c)],
                send_sem=give_sem.at[k, c], recv_sem=take_sem.at[k, c],
                device_id={"group": peer}, device_id_type=mesh_id)
            copy.start()
            passed.append((c, k, copy))
    for c in range(chunks):
        total = field[pl.ds(pl.multiple_of(group * rows, rows), rows), columns(c)]
        for at, k, copy in passed:
            if at == c:
                copy.wait_recv()
                total = total + take[k, :, columns(c)].astype(jnp.float32)
        out_ref[0, :, columns(c)] = -total
    for _, _, copy in passed:
        copy.wait_send()
    for copy in sent[1:]:
        copy.wait_send()
    label_copy.wait_send()


def shards(trial, orbitals, labels, kernel_mask):
    n = trial.shape[1]
    bands, groups = lax.axis_size("band"), lax.axis_size("group")
    rows = n // groups
    chunks = n // (STACK * STACK)
    peers = groups - 1
    hbm = pl.BlockSpec(memory_space=pltpu.HBM)
    dma = pltpu.SemaphoreType.DMA
    return pl.pallas_call(
        functools.partial(exchange_kernel, n, bands, groups),
        out_shape=jax.ShapeDtypeStruct((1, rows, n * n), jnp.float32),
        in_specs=[hbm, hbm, pl.BlockSpec(memory_space=pltpu.SMEM), hbm],
        out_specs=pl.BlockSpec(memory_space=pltpu.VMEM),
        scratch_shapes=[
            pltpu.VMEM((STACK * n, STACK * n), jnp.bfloat16),
            pltpu.VMEM((n, n * n), jnp.bfloat16),
            pltpu.VMEM((n, n * n), jnp.bfloat16),
            pltpu.VMEM((n, n * n), jnp.bfloat16),
            pltpu.VMEM((n, n * n), jnp.int32),
            pltpu.VMEM((n * n // STACK, STACK * n), jnp.bfloat16),
            pltpu.VMEM((n * n // STACK, STACK * n), jnp.bfloat16),
            pltpu.VMEM((n // 2 * (n + PAD) + n, 2 * n), jnp.float32),
            pltpu.VMEM((n // 2 * (n + PAD) + n, 2 * n), jnp.float32),
            pltpu.VMEM((n // 2 * (n + PAD) + n, 2 * n), jnp.float32),
            pltpu.VMEM((n, n * n), jnp.float32),
            pltpu.VMEM((8, STACK * n), jnp.int32),
            pltpu.VMEM((8, STACK * n), jnp.int32),
            pltpu.VMEM((peers, rows, n * n), jnp.bfloat16),
            pltpu.VMEM((peers, rows, n * n), jnp.bfloat16),
            dma((3,)), dma((chunks,)), dma((chunks,)), dma, dma, dma((peers, chunks)), dma((peers, chunks)),
        ],
        compiler_params=pltpu.CompilerParams(
            collective_id=0, has_side_effects=True, vmem_limit_bytes=53 * 1024 * 1024),
        name="exchange",
    )(trial, orbitals, labels, kernel_mask)


def solution(mesh):
    in_specs = (P("band", None, None), P(("band", "group"), None, None), P(("band", "group")), P())
    out_specs = P("band", "group", None)
    return jax.shard_map(shards, mesh=mesh, in_specs=in_specs, out_specs=out_specs, check_vma=False)
```
